512 devices in a mesh: zone: 32 (over z, core), line: 16 (over y, x).
Axes of the slice: x: 4, y: 4, z: 16, core: 2. Of those that a mesh axis runs over, the one named last changes fastest.
Arguments:
- flow_state: float32 [32, 5, 64, 128, 128], P('zone', None, 'line'), may hold values from -6 to 6
- derivative: float32 [2, 128, 128], replicated, may hold values from -0.5 to 0.5
- derivative_z: float32 [64, 64], replicated, may hold values from -0.75 to 0.75
- line_inverse: float32 [32, 2, 5, 128, 128], P('zone')
- line_inverse_z: float32 [32, 5, 64, 64], P('zone')
- mixers: float32 [32, 7, 5, 5], P('zone')
- zone_size: int32 [32], P('zone'), may hold values from 1 to 64, 682 in all
- receiver_line: int32 [32, 16, 128], P('zone', 'line'), may hold values from 0 to 511, as said below
- donor_group: int32 [32, 16, 128, 1], P('zone', 'line'), may hold values from 0 to 31; in each aligned block of 128 rows (0 to 127, 128 to 255, ..., all dimensions but the last counted through in order) at most 10 rows name the same one
- donor_line: int32 [32, 16, 128, 2], P('zone', 'line'), may hold values from 0 to 511
- stencil_weight: float32 [32, 16, 128], P('zone', 'line'), may hold values from 0 to 1
Outputs:
- state_update: float32 [32, 5, 64, 128, 128], P('zone', None, 'line')
The draws below stay inside these ranges and needn't reach their ends.
Inputs may be any that keep to these rules, and one draw needn't show every extreme that they name: `receiver_line`: within one line block of one group the 128 receiver lines are distinct. `donor_group`: among the 128 slots of one line block of one group no donor group is named more than 10 times; in some line blocks some donor group is named exactly 10 times. `zone_size`: the sizes of all groups add up to 682, and the largest is 64.
All inputs are finite; a program needn't handle non-finite values.
Results may differ from the reference program's by a relative error of at most 0.0003.
Values sent between devices are 32-bit elements; how exact they have to be, the bound alone decides.
A program may use at most 64 MiB of HBM per device.

```python
import math
import jax
import jax.numpy as jnp
import numpy as np
from jax import lax

EDGE_CELLS = 128
ZCELLS = 64
RECEIVERS = 128
GROUPS = 32
BLOCKS = 16
BLOCK_LINES = 512
CAPACITY = 10


def draw_line_inverse(key, part):
    shape = (GROUPS, 2, 5, EDGE_CELLS, EDGE_CELLS)
    noise = jax.random.normal(key, shape, jnp.float32)
    return 0.8 * jnp.eye(EDGE_CELLS, dtype=jnp.float32) + 0.4 / math.sqrt(EDGE_CELLS) * noise


def draw_line_inverse_z(key, part):
    shape = (GROUPS, 5, ZCELLS, ZCELLS)
    noise = jax.random.normal(key, shape, jnp.float32)
    return 0.8 * jnp.eye(ZCELLS, dtype=jnp.float32) + 0.4 / math.sqrt(ZCELLS) * noise


def draw_mixers(key, part):
    noise = jax.random.normal(key, (GROUPS, 7, 5, 5), jnp.float32)
    return 0.8 * jnp.eye(5, dtype=jnp.float32) + 0.15 * noise


def draw_receiver_line(key, part):
    keys = jax.random.split(key, GROUPS * BLOCKS)
    chosen = jax.vmap(lambda single: jax.random.permutation(single, BLOCK_LINES)[:RECEIVERS])(keys)
    return chosen.reshape(GROUPS, BLOCKS, RECEIVERS).astype(jnp.int32)


def touch_ends(values, stream_key, low, high):
    extent = values.shape
    place = [jax.random.randint(jax.random.fold_in(stream_key, axis), (), 0, extent[axis]) for axis in range(len(extent))]
    values = values.at[tuple(place)].set(low)
    longest = extent.index(max(extent))
    place[longest] = (place[longest] + 1) % extent[longest]
    return values.at[tuple(place)].set(high)


def block_scale(own_key, shape, shards, smallest, largest):
    loudness, own = 1.0, jax.random.fold_in(own_key, 6)
    for position, parts in shards:
        draws = jnp.exp(jax.random.uniform(jax.random.fold_in(own, position), (parts,), jnp.float32, smallest / len(shards), largest / len(shards)))
        loudness = loudness * jnp.repeat(draws, shape[position] // parts).reshape([-1 if axis == position else 1 for axis in range(len(shape))])
    return loudness


def length_profile(number_of, total, bound, skew):
    portions = [(1 << 20) // math.isqrt(rank ** skew) + 1 for rank in range(2, number_of + 1)]
    rest, holding = total - bound - (number_of - 1), [1] * (number_of - 1)
    while rest > 0:
        candidates = [i for i in range(number_of - 1) if holding[i] < bound]
        whole, budget = sum([portions[i] for i in candidates]), rest
        for i in candidates:
            extra = min(bound - holding[i], max(1, budget * portions[i] // whole), rest)
            holding[i] = holding[i] + extra
            rest = rest - extra
    return np.array([bound] + holding)


def ragged_sizes(key, count, total, limit, skew):
    if count == 2:
        one = jax.random.randint(key, (), max(1, total - limit), min(limit, total - 1) + 1)
        return jnp.stack([one, total - one])
    tallies = jnp.asarray(length_profile(count, total, limit, skew), jnp.int32)
    pairs = (count - 1) // 2
    giver, receiver = tallies[1:1 + 2 * pairs:2], tallies[2:2 + 2 * pairs:2]
    room = jnp.minimum(giver - 1, limit - receiver)
    shifted = jax.random.randint(jax.random.fold_in(key, 1), (pairs,), 0, 1 << 20) % (room + 1)
    tallies = tallies.at[1:1 + 2 * pairs:2].set(giver - shifted).at[2:2 + 2 * pairs:2].set(receiver + shifted)
    return tallies[jax.random.permutation(jax.random.fold_in(key, 2), count)]


def routed_block(key, own, number, rows, amount, top, reach, slope):
    order = jax.random.permutation(key, amount)
    heavy_load, ordinary = load_shares(amount, rows * top, reach, slope, True), load_shares(amount, rows * top, reach, slope, False)
    places = jnp.arange(amount)

    def named(lengths, rotation):
        used = int((lengths > 0).sum())
        fixed = max(1, used // 4)
        passed = fixed + (places - fixed + rotation * (used - fixed)) % max(1, amount - fixed)
        return jnp.zeros((amount,), jnp.int32).at[order[jnp.where(places < fixed, places, passed)]].set(jnp.asarray(lengths, jnp.int32))

    lengths = jnp.where(number % 4 == 0, named(heavy_load, number // 4), named(ordinary, number - number // 4 - 1))
    mixed = jax.random.permutation(jax.random.fold_in(own, 3), amount)
    source_of, sink = mixed[0:amount // 2 * 2:2], mixed[1:amount // 2 * 2:2]
    slack = jnp.minimum(lengths[source_of] - 1, reach - lengths[sink]) // 2
    slack = jnp.where((source_of == order[0]) | (sink == order[0]) | (lengths[sink] == 0), 0, jnp.maximum(slack, 0))
    passed = jax.random.randint(jax.random.fold_in(own, 4), (amount // 2,), 0, 1 << 20) % (slack + 1)
    lengths = lengths.at[source_of].add(-passed).at[sink].add(passed)
    labels = jnp.searchsorted(jnp.cumsum(lengths), jnp.arange(rows * top), side="right").astype(jnp.int32)
    listing = labels.reshape(top, rows).T
    listing = listing[jax.random.permutation(jax.random.fold_in(own, 1), rows)]
    rotation = jax.random.randint(jax.random.fold_in(own, 2), (rows, 1), 0, top)
    return jnp.take_along_axis(listing, (jnp.arange(top)[None, :] + rotation) % top, axis=1)


def load_shares(number_of, total, bound, slope, full):
    portions = [(1 << 20) // math.isqrt(rank ** slope) + 1 for rank in range(1, number_of + 1)]
    largest = bound if full else min(bound, max(-(-total // number_of), total * portions[0] // sum(portions)))
    least = 1 if total - largest >= number_of - 1 else 0
    given, surplus = [largest] + [least] * (number_of - 1), total - largest - least * (number_of - 1)
    while surplus > 0:
        free = [i for i in range(1, number_of) if given[i] < largest] or [i for i in range(1, number_of) if given[i] < bound]
        pool, budget = sum([portions[i] for i in free]), surplus
        for i in free:
            addition = min(bound - given[i], max(1, budget * portions[i] // pool), surplus)
            given[i] = given[i] + addition
            surplus = surplus - addition
    return np.array(given)


def scatter_about(own_key, shape, scale, reach, pieces=(), kind=jnp.bfloat16):
    entries = jax.random.normal(own_key, shape, jnp.float32) * scale
    if len(pieces) > 0:
        entries = block_scale(own_key, shape, pieces, -0.22, 0.18) * entries
    return jnp.clip(entries, min=-reach, max=reach).astype(kind)


def setup_inputs(seed: int = 0) -> dict:
    key_of = jax.random.split(jax.random.key(seed), 12)
    flow_state = scatter_about(key_of[0], (GROUPS, 5, ZCELLS, EDGE_CELLS, EDGE_CELLS), 1.0, 6.0, ((0, 32), (2, 16)), jnp.float32)
    derivative = scatter_about(key_of[1], (2, EDGE_CELLS, EDGE_CELLS), EDGE_CELLS ** -0.5, 0.5, (), jnp.float32)
    derivative_z = scatter_about(key_of[2], (ZCELLS, ZCELLS), ZCELLS ** -0.5, 0.75, (), jnp.float32)
    line_inverse = draw_line_inverse(jax.random.fold_in(key_of[11], 71), 0)
    line_inverse_z = draw_line_inverse_z(jax.random.fold_in(key_of[11], 71), 0)
    mixers = draw_mixers(jax.random.fold_in(key_of[11], 71), 0)
    zone_size = ragged_sizes(key_of[6], GROUPS, GROUPS * ZCELLS // 3, ZCELLS, 2).astype(jnp.int32)
    receiver_line = draw_receiver_line(jax.random.fold_in(key_of[11], 71), 0)
    donor_group_keys = jax.random.split(jax.random.fold_in(key_of[8], 1), GROUPS * BLOCKS * RECEIVERS // RECEIVERS)
    donor_group_turns = jax.random.permutation(jax.random.fold_in(key_of[8], 3), GROUPS * BLOCKS * RECEIVERS // RECEIVERS)
    donor_group = jax.vmap(lambda own, number: routed_block(jax.random.fold_in(key_of[8], 2), own, number, RECEIVERS, GROUPS, 1, CAPACITY, 2))(donor_group_keys, donor_group_turns).reshape((GROUPS, BLOCKS, RECEIVERS, 1))
    donor_line = touch_ends(jax.random.randint(key_of[9], (GROUPS, BLOCKS, RECEIVERS, 2), 0, BLOCK_LINES), jax.random.fold_in(key_of[9], 1), 0, BLOCK_LINES - 1).astype(jnp.int32)
    stencil_weight = jnp.clip(1.0 * jax.random.uniform(key_of[10], (GROUPS, BLOCKS, RECEIVERS), jnp.float32) ** block_scale(key_of[10], (GROUPS, BLOCKS, RECEIVERS), ((0, 32), (1, 16)), -0.2, 0.2), 0.0, 1.0)
    return {"flow_state": flow_state, "derivative": derivative, "derivative_z": derivative_z, "line_inverse": line_inverse, "line_inverse_z": line_inverse_z, "mixers": mixers, "zone_size": zone_size, "receiver_line": receiver_line, "donor_group": donor_group, "donor_line": donor_line, "stencil_weight": stencil_weight}


highest = lax.Precision.HIGHEST


def apply_mixer(matrix, fields):
    return jnp.einsum('mv,vkji->mkji', matrix, fields, precision=highest)


def reference(flow_state, derivative, derivative_z, line_inverse, line_inverse_z, mixers, zone_size, receiver_line, donor_group, donor_line, stencil_weight):
    line_view = flow_state.reshape(GROUPS, 5, BLOCKS, BLOCK_LINES, EDGE_CELLS)
    block_index = jnp.arange(BLOCKS, dtype=jnp.int32)[:, None]

    def one_group(group):
        fields = flow_state[group]
        mixing = mixers[group]
        inverses = line_inverse[group]
        inverse_z = line_inverse_z[group]
        term_x = jnp.einsum('vkji,mi->vkjm', apply_mixer(mixing[0], fields), derivative[0], precision=highest)
        term_y = jnp.einsum('vkji,mj->vkmi', apply_mixer(mixing[1], fields), derivative[1], precision=highest)
        term_z = jnp.einsum('vkji,mk->vmji', apply_mixer(mixing[2], fields), derivative_z, precision=highest)
        active = jnp.arange(ZCELLS, dtype=jnp.int32) < zone_size[group]
        residual = jnp.where(active[None, :, None, None], -(term_x + term_y + term_z), 0.0)
        donors = donor_group[group][:, :, 0]
        first_rows = line_view[donors, :, block_index, donor_line[group][:, :, 0]]
        second_rows = line_view[donors, :, block_index, donor_line[group][:, :, 1]]
        weight = stencil_weight[group][:, :, None, None]
        interp = weight * first_rows + (1.0 - weight) * second_rows
        receivers = receiver_line[group]
        own_rows = line_view[group][:, block_index, receivers]
        source = jnp.zeros((5, BLOCKS, BLOCK_LINES, EDGE_CELLS), flow_state.dtype)
        source = source.at[:, block_index, receivers].set(jnp.transpose(interp, (2, 0, 1, 3)) - own_rows)
        rhs = residual + source.reshape(fields.shape)
        first = apply_mixer(mixing[3], rhs)
        first = jnp.einsum('vkji,vmk->vmji', first, inverse_z, precision=highest)
        first = apply_mixer(mixing[4], first)
        second = jnp.einsum('vkji,vmj->vkmi', first, inverses[1], precision=highest)
        second = apply_mixer(mixing[5], second)
        final = jnp.einsum('vkji,vmi->vkjm', second, inverses[0], precision=highest)
        return apply_mixer(mixing[6], final)

    return lax.map(one_group, jnp.arange(GROUPS, dtype=jnp.int32))
```

```python
import functools

import jax
import jax.numpy as jnp
from jax import lax
from jax.experimental import pallas as pl
from jax.experimental.pallas import tpu as pltpu
from jax.sharding import PartitionSpec as P

f32 = jnp.float32
bf16 = jnp.bfloat16
VARS = 5
LANES = 128
CHUNKS = ((0, 2), (2, 4), (4, 5))


def split(x):
    high = x.astype(bf16)
    return high, (x - high.astype(f32)).astype(bf16)


def dot(a, b):
    return jnp.dot(a, b, preferred_element_type=f32)


def left_rows(w):
    high, low = split(w)
    return jnp.concatenate(
        [jnp.concatenate([high, high], 1), jnp.concatenate([low, jnp.zeros_like(low)], 1)], 0
    )


def left_mul(w, x):
    high, low = split(x)
    both = dot(left_rows(w), jnp.concatenate([high, low], 0))
    half = w.shape[0]
    return both[:half] + both[half:]


def right_columns(w):
    high, low = split(w)
    return jnp.concatenate(
        [jnp.concatenate([high, low], 1), jnp.concatenate([high, jnp.zeros_like(low)], 1)], 0
    )


def right_mul(x, columns):
    high, low = split(x)
    both = dot(jnp.concatenate([high, low], 1), columns)
    half = columns.shape[1] // 2
    return both[:, :half] + both[:, half:]


def pick(rows, x):
    first, rest = split(x)
    rest = x - first.astype(f32)
    second = rest.astype(bf16)
    third = (rest - second.astype(f32)).astype(bf16)
    return (dot(rows, first) + dot(rows, second)) + dot(rows, third)


def iota(shape, axis):
    return lax.broadcasted_iota(jnp.int32, shape, axis)


def kernel(
    capacity,
    q, deriv, deriv_z, inverse, inverse_z, mix, size, receivers, donors, pairs, weights,
    out,
    req_out, req_in, q_strips, q_both, q_turned, ddx, ddy, part, part_strips, ret_out, ret_in, choose, place,
    part_turned, zed, mixed, solved, turned_back, back, step_a, step_b,
    local_sem, req_sem, q_sem, ret_send, ret_recv, part_send, part_recv, back_send, back_recv,
):
    groups, blocks = lax.axis_size("zone"), lax.axis_size("line")
    zone, line = lax.axis_index("zone"), lax.axis_index("line")
    planes, edge = q.shape[1], q.shape[2]
    rows = planes * edge
    depth = planes * blocks
    width = edge // blocks
    slots = receivers.shape[1]
    piece = planes * width
    named = groups * capacity
    padded = ret_in.shape[1]

    def over_zone(body):
        def step(s, carry):
            body(lax.rem(zone + s, groups))
            return carry

        lax.fori_loop(1, groups, step, 0)

    def over_line(body):
        def step(s, carry):
            body(lax.rem(line + s, blocks))
            return carry

        lax.fori_loop(1, blocks, step, 0)

    def strips(x):
        x = x.reshape(planes, blocks, width, LANES)
        return jnp.swapaxes(x, 0, 1).reshape(blocks, piece, LANES)

    def level(t):
        return pl.ds(pl.multiple_of(t * piece, piece), piece)

    others = pl.ds(0, (blocks - 1) * piece)

    def wait_for(ref, sem):
        pltpu.make_async_copy(ref, ref, sem).wait()

    barrier = pltpu.get_barrier_semaphore()
    over_zone(lambda g: pl.semaphore_signal(barrier, inc=1, device_id={"zone": g}))
    over_line(lambda t: pl.semaphore_signal(barrier, inc=1, device_id={"line": t}))

    diagonal = iota((slots, slots), 0) == iota((slots, slots), 1)

    def column(row):
        return jnp.sum(jnp.where(diagonal, row, 0.0), axis=1, keepdims=True)

    donor_row = donors[...].astype(f32)
    donor = column(donor_row)
    same_before = (donor == donor_row) & (iota((slots, slots), 1) < iota((slots, slots), 0))
    position = jnp.sum(jnp.where(same_before, 1.0, 0.0), axis=1, keepdims=True)
    lane = iota((slots, LANES), 1).astype(f32)
    line_pair = pairs[...].astype(f32)
    told = (
        jnp.where(lane == position, column(line_pair[0:1]), 0.0)
        + jnp.where(lane == position + capacity, column(line_pair[1:2]), 0.0)
        + jnp.where(lane == position + 2 * capacity, column(weights[...]), 0.0)
    )
    asks = jnp.where(iota((groups, slots), 0).astype(f32) == donor_row, 1.0, 0.0).astype(bf16)
    req_out[...] = pick(asks, told).reshape(groups, 1, LANES)

    pl.semaphore_wait(barrier, groups + blocks - 2)

    def send_request(g):
        pltpu.make_async_remote_copy(
            src_ref=req_out.at[g], dst_ref=req_in.at[zone],
            send_sem=req_sem.at[0], recv_sem=req_sem.at[1], device_id={"zone": g},
        ).start()

    over_zone(send_request)
    own_request = pltpu.make_async_copy(req_out.at[zone], req_in.at[zone], local_sem.at[0])
    own_request.start()

    def cut_state(v, carry):
        q_strips[v] = strips(q[v])
        return carry

    lax.fori_loop(0, VARS, cut_state, 0)

    def send_state(t):
        pltpu.make_async_remote_copy(
            src_ref=q_strips.at[:, t], dst_ref=q_turned.at[:, level(line)],
            send_sem=q_sem.at[0], recv_sem=q_sem.at[1], device_id={"line": t},
        ).start()

    over_line(send_state)
    own_state = pltpu.make_async_copy(
        q_strips.at[:, line], q_turned.at[:, level(line)], local_sem.at[1]
    )
    own_state.start()

    def part_state(v, carry):
        high, low = split(q[v].reshape(rows, LANES))
        q_both[v] = jnp.concatenate([high, low], 1)
        return carry

    lax.fori_loop(0, VARS, part_state, 0)

    own_request.wait()
    wait_for(req_in.at[pl.ds(0, groups - 1)], req_sem.at[1])
    slot = iota((named, groups), 0)
    low_end = iota((named, groups), 1) * capacity
    spread = jnp.where((slot >= low_end) & (slot < low_end + capacity), 1.0, 0.0).astype(bf16)
    asked = pick(spread, req_in[...].reshape(groups, LANES))
    slot = iota((named, LANES), 0)
    turn = slot - capacity * ((slot * (65536 // capacity + 1)) >> 16)
    lane = iota((named, LANES), 1)

    def field(n):
        return jnp.sum(jnp.where(lane == turn + n * capacity, asked, 0.0), axis=1, keepdims=True)

    first_line, second_line, share = field(0), field(1), field(2)
    cell_line = iota((named, rows), 1).astype(f32)
    high, low = split(
        jnp.where(cell_line == first_line, share, 0.0)
        + jnp.where(cell_line == second_line, 1.0 - share, 0.0)
    )
    choose[0:named] = high
    choose[named:] = low

    def interpolate(v, carry):
        both = dot(choose[...], q_both[v])
        value = (both[:named, :LANES] + both[:named, LANES:]) + both[named:, :LANES]
        ret_out[v] = value.reshape(named, 1, LANES)
        return carry

    own_lines = []
    for c, (start, stop) in enumerate(CHUNKS):
        lax.fori_loop(start, stop, interpolate, 0)

        def send_lines(g):
            pltpu.make_async_remote_copy(
                src_ref=ret_out.at[start:stop, pl.ds(g * capacity, capacity)],
                dst_ref=ret_in.at[start:stop, pl.ds(zone * capacity, capacity)],
                send_sem=ret_send.at[c], recv_sem=ret_recv.at[c], device_id={"zone": g},
            ).start()

        over_zone(send_lines)
        mine = pl.ds(zone * capacity, capacity)
        copy = pltpu.make_async_copy(
            ret_out.at[start:stop, mine], ret_in.at[start:stop, mine], local_sem.at[2 + c]
        )
        copy.start()
        own_lines.append(copy)

    first_columns = right_columns(deriv[0].T)
    second_rows = left_rows(deriv[1])

    def derive(v, carry):
        both = dot(q_both[v], first_columns)
        ddx[v] = both[:, :LANES] + both[:, LANES:]
        state = q_both[v]
        stacked = jnp.concatenate(
            [
                jnp.concatenate([state[k * edge:(k + 1) * edge, n:n + LANES] for k in range(planes)], 1)
                for n in (0, LANES)
            ],
            0,
        )
        both = dot(second_rows, stacked)
        both = both[:edge] + both[edge:]
        for k in range(planes):
            ddy[v, k * edge:(k + 1) * edge] = both[:, k * LANES:(k + 1) * LANES]
        return carry

    lax.fori_loop(0, VARS, derive, 0)
    tile = min(32, edge)

    def residual(n, carry):
        at = pl.ds(pl.multiple_of(n * tile, tile), tile)
        plane = n // (edge // tile)
        active = line * planes + plane < size[0]
        x = [ddx[v, at] for v in range(VARS)]
        y = [ddy[v, at] for v in range(VARS)]
        for a in range(VARS):
            total = mix[0, a, 0] * x[0] + mix[1, a, 0] * y[0]
            for v in range(1, VARS):
                total += mix[0, a, v] * x[v] + mix[1, a, v] * y[v]
            part[a, at] = jnp.where(active, -total, 0.0)
        return carry

    lax.fori_loop(0, rows // tile, residual, 0)

    slot_of = donor * capacity + position
    here = jnp.sum(
        jnp.where(
            iota((slots, padded), 1).astype(f32) == slot_of,
            column(receivers[...].astype(f32)) + 1.0,
            0.0,
        ),
        axis=0,
        keepdims=True,
    ) - 1.0
    place[...] = jnp.where(iota((rows, padded), 0).astype(f32) == here, 1.0, 0.0).astype(bf16)
    is_receiver = jnp.sum(
        jnp.where(iota((rows, slots), 0) == receivers[...], 1.0, 0.0), axis=1, keepdims=True
    )
    if padded > named:
        ret_in[:, named:] = jnp.zeros((VARS, padded - named, 1, LANES), f32)

    own_state.wait()
    wait_for(q_turned.at[:, others], q_sem.at[1])

    def whole_lines(ref, v):
        return jnp.concatenate(
            [ref[v, pl.ds(j, depth, stride=width), :] for j in range(width)], 1
        )

    def derive_z(v, carry):
        zed[v] = left_mul(deriv_z[...], whole_lines(q_turned, v))
        return carry

    lax.fori_loop(0, VARS, derive_z, 0)
    active_all = iota((depth, LANES), 0) < size[0]

    def residual_z(j, carry):
        at = pl.ds(pl.multiple_of(j * LANES, LANES), LANES)
        z = [zed[v, :, at] for v in range(VARS)]
        for a in range(VARS):
            total = mix[2, a, 0] * z[0]
            for v in range(1, VARS):
                total += mix[2, a, v] * z[v]
            mixed[a, :, at] = jnp.where(active_all, -total, 0.0)
        return carry

    lax.fori_loop(0, width, residual_z, 0)

    def add_source(v, carry):
        high, low = split(ret_in[v].reshape(padded, LANES))
        both = dot(place[...], jnp.concatenate([high, low], 1))
        own = is_receiver * q[v].reshape(rows, LANES)
        part_strips[v] = strips(part[v] + (both[:, :LANES] + both[:, LANES:] - own))

        def send_part(t):
            pltpu.make_async_remote_copy(
                src_ref=part_strips.at[v, t],
                dst_ref=part_turned.at[v, level(line)],
                send_sem=part_send.at[v], recv_sem=part_recv.at[v], device_id={"line": t},
            ).start()

        over_line(send_part)
        part_turned[v, level(line)] = part_strips[v, line]
        return carry

    for c, (start, stop) in enumerate(CHUNKS):
        own_lines[c].wait()
        wait_for(ret_in.at[start:stop, pl.ds(0, named - capacity)], ret_recv.at[c])
        lax.fori_loop(start, stop, add_source, 0)

    for v in range(VARS):
        wait_for(part_turned.at[v, others], part_recv.at[v])

    def to_first(j, carry):
        at = pl.ds(pl.multiple_of(j * LANES, LANES), LANES)
        r = [part_turned[v, pl.ds(j, depth, stride=width), :] + mixed[v, :, at] for v in range(VARS)]
        for a in range(VARS):
            total = mix[3, a, 0] * r[0]
            for v in range(1, VARS):
                total += mix[3, a, v] * r[v]
            zed[a, :, at] = total
        return carry

    lax.fori_loop(0, width, to_first, 0)

    def solve_z(v, carry):
        solved[v] = left_mul(inverse_z[v], zed[v])
        return carry

    lax.fori_loop(0, VARS, solve_z, 0)

    def send_back(a, carry):
        for j in range(width):
            at = slice(j * LANES, (j + 1) * LANES)
            total = mix[4, a, 0] * solved[0, :, at]
            for v in range(1, VARS):
                total += mix[4, a, v] * solved[v, :, at]
            turned_back[a, pl.ds(j, depth, stride=width), :] = total

        def send(t):
            pltpu.make_async_remote_copy(
                src_ref=turned_back.at[a, level(t)],
                dst_ref=back.at[a, line],
                send_sem=back_send.at[a], recv_sem=back_recv.at[a], device_id={"line": t},
            ).start()

        over_line(send)
        back[a, line] = turned_back[a, level(line)]
        return carry

    lax.fori_loop(0, VARS, send_back, 0)

    def plane_of(v, k):
        return back[v, :, k * width:(k + 1) * width, :].reshape(edge, LANES)

    def solve_y(v, carry):
        wait_for(turned_back.at[v, others], back_recv.at[v])
        both = left_mul(inverse[1, v], jnp.concatenate([plane_of(v, k) for k in range(planes)], 1))
        for k in range(planes):
            step_a[v, k * edge:(k + 1) * edge] = both[:, k * LANES:(k + 1) * LANES]
        return carry

    lax.fori_loop(0, VARS, solve_y, 0)

    def mix_over(m, source, store):
        def body(n, carry):
            at = pl.ds(pl.multiple_of(n * tile, tile), tile)
            x = [source[v, at] for v in range(VARS)]
            for a in range(VARS):
                total = mix[m, a, 0] * x[0]
                for v in range(1, VARS):
                    total += mix[m, a, v] * x[v]
                store(a, n, at, total)
            return carry

        lax.fori_loop(0, rows // tile, body, 0)

    def keep(a, n, at, total):
        step_b[a, at] = total

    def give(a, n, at, total):
        inside = lax.rem(n, edge // tile) * tile
        out[a, n // (edge // tile), pl.ds(pl.multiple_of(inside, tile), tile)] = total

    mix_over(5, step_a, keep)

    def solve_x(v, carry):
        step_a[v] = right_mul(step_b[v], right_columns(inverse[0, v].T))
        return carry

    lax.fori_loop(0, VARS, solve_x, 0)
    mix_over(6, step_a, give)

    wait_for(req_in.at[pl.ds(0, groups - 1)], req_sem.at[0])
    wait_for(q_turned.at[:, others], q_sem.at[0])
    for c, (start, stop) in enumerate(CHUNKS):
        wait_for(ret_out.at[start:stop, pl.ds(0, named - capacity)], ret_send.at[c])
    for v in range(VARS):
        wait_for(part_turned.at[v, others], part_send.at[v])
        wait_for(turned_back.at[v, others], back_send.at[v])


def local(
    flow_state, derivative, derivative_z, line_inverse, line_inverse_z, mixers, zone_size,
    receiver_line, donor_group, donor_line, stencil_weight,
):
    groups, blocks = lax.axis_size("zone"), lax.axis_size("line")
    planes, edge = flow_state.shape[2], flow_state.shape[3]
    slots = receiver_line.shape[2]
    capacity = max(2, 5 * slots // (2 * groups))
    rows, depth, width = planes * edge, planes * blocks, edge // blocks
    named = groups * capacity
    padded = -(-named // LANES) * LANES
    dma = pltpu.SemaphoreType.DMA
    vmem = pl.BlockSpec(memory_space=pltpu.VMEM)
    smem = pl.BlockSpec(memory_space=pltpu.SMEM)
    result = pl.pallas_call(
        functools.partial(kernel, capacity),
        out_shape=jax.ShapeDtypeStruct((VARS, planes, edge, LANES), f32),
        in_specs=[vmem] * 5 + [smem] * 2 + [vmem] * 4,
        out_specs=vmem,
        scratch_shapes=[
            pltpu.VMEM((groups, 1, LANES), f32),
            pltpu.VMEM((groups, 1, LANES), f32),
            pltpu.VMEM((VARS, blocks, planes * width, LANES), f32),
            pltpu.VMEM((VARS, rows, 2 * LANES), bf16),
            pltpu.VMEM((VARS, depth * width, LANES), f32),
            pltpu.VMEM((VARS, rows, LANES), f32),
            pltpu.VMEM((VARS, rows, LANES), f32),
            pltpu.VMEM((VARS, rows, LANES), f32),
            pltpu.VMEM((VARS, blocks, planes * width, LANES), f32),
            pltpu.VMEM((VARS, named, 1, LANES), f32),
            pltpu.VMEM((VARS, padded, 1, LANES), f32),
            pltpu.VMEM((2 * named, rows), bf16),
            pltpu.VMEM((rows, padded), bf16),
            pltpu.VMEM((VARS, depth * width, LANES), f32),
            pltpu.VMEM((VARS, depth, width * LANES), f32),
            pltpu.VMEM((VARS, depth, width * LANES), f32),
            pltpu.VMEM((VARS, depth, width * LANES), f32),
            pltpu.VMEM((VARS, depth * width, LANES), f32),
            pltpu.VMEM((VARS, blocks, planes * width, LANES), f32),
            pltpu.VMEM((VARS, rows, LANES), f32),
            pltpu.VMEM((VARS, rows, LANES), f32),
            dma((2 + len(CHUNKS),)),
            dma((2,)),
            dma((2,)),
            dma((len(CHUNKS),)),
            dma((len(CHUNKS),)),
            dma((VARS,)),
            dma((VARS,)),
            dma((VARS,)),
            dma((VARS,)),
        ],
        compiler_params=pltpu.CompilerParams(
            collective_id=0, has_side_effects=True, vmem_limit_bytes=48 * 2**20
        ),
    )(
        flow_state[0], derivative, derivative_z, line_inverse[0], line_inverse_z[0], mixers[0],
        zone_size, receiver_line[0], donor_group[0, :, :, 0], donor_line[0, 0].T,
        stencil_weight[0],
    )
    return result[None]


def solution(mesh):
    placed = (
        P("zone", None, "line", None, None),
        P(),
        P(),
        P("zone", None, None, None, None),
        P("zone", None, None, None),
        P("zone", None, None, None),
        P("zone"),
        P("zone", "line", None),
        P("zone", "line", None, None),
        P("zone", "line", None, None),
        P("zone", "line", None),
    )
    return jax.shard_map(
        local,
        mesh=mesh,
        in_specs=placed,
        out_specs=P("zone", None, "line", None, None),
        check_vma=False,
    )
```

```python
import functools

import jax
import jax.numpy as jnp
from jax import lax
from jax.experimental import pallas as pl
from jax.experimental.pallas import tpu as pltpu
from jax.sharding import PartitionSpec as P

f32 = jnp.float32
bf16 = jnp.bfloat16
VARS = 5
LANES = 128


def split(x):
    high = x.astype(bf16)
    return high, (x - high.astype(f32)).astype(bf16)


def dot(a, b):
    return jnp.dot(a, b, preferred_element_type=f32)


def left_rows(w):
    high, low = split(w)
    return jnp.concatenate(
        [jnp.concatenate([high, high], 1), jnp.concatenate([low, jnp.zeros_like(low)], 1)], 0
    )


def left_mul(w, x):
    high, low = split(x)
    both = dot(left_rows(w), jnp.concatenate([high, low], 0))
    half = w.shape[0]
    return both[:half] + both[half:]


def right_columns(w):
    high, low = split(w)
    return jnp.concatenate(
        [jnp.concatenate([high, low], 1), jnp.concatenate([high, jnp.zeros_like(low)], 1)], 0
    )


def right_mul(x, columns):
    high, low = split(x)
    both = dot(jnp.concatenate([high, low], 1), columns)
    half = columns.shape[1] // 2
    return both[:, :half] + both[:, half:]


def pick(rows, x):
    first, rest = split(x)
    rest = x - first.astype(f32)
    second = rest.astype(bf16)
    third = (rest - second.astype(f32)).astype(bf16)
    return (dot(rows, first) + dot(rows, second)) + dot(rows, third)


def iota(shape, axis):
    return lax.broadcasted_iota(jnp.int32, shape, axis)


def kernel(
    capacity,
    q_hbm, deriv_hbm, deriv_z_hbm, inverse_hbm, inverse_z_hbm, mixers, size,
    receivers_hbm, donors_hbm, pairs_hbm, weights_hbm,
    out,
    q, deriv, deriv_z, inverse, inverse_z, receivers, donors, pairs, weights,
    req_out, req_in, q_strips, q_both, q_turned, ddx, ddy, part, part_strips, is_receiver,
    lines, ret_out, ret_in, choose, place,
    part_turned, zed, mixed, turned_back, back, step_a, step_b,
    load_sem, local_sem, req_sem, q_sem,
    ret_send, ret_recv, part_send, part_recv, back_send, back_recv,
):
    groups, blocks = lax.axis_size("zone"), lax.axis_size("line")
    zone, line = lax.axis_index("zone"), lax.axis_index("line")

    def mix(m, a, v):
        return mixers[a * VARS + v, 0, m]

    moves = [
        pltpu.make_async_copy(source, target, load_sem.at[n])
        for n, (source, target) in enumerate((
            (donors_hbm, donors), (pairs_hbm, pairs), (weights_hbm, weights), (q_hbm, q),
            (receivers_hbm, receivers), (deriv_hbm, deriv), (deriv_z_hbm, deriv_z),
            (inverse_z_hbm, inverse_z), (inverse_hbm, inverse),
        ))
    ]
    for move in moves:
        move.start()
    planes, edge = q.shape[1], q.shape[2]
    rows = planes * edge
    depth = planes * blocks
    width = edge // blocks
    slots = receivers.shape[1]
    piece = planes * width
    named = groups * capacity
    padded = ret_in.shape[1]

    def over_zone(body):
        def step(s, carry):
            body(lax.rem(zone + s, groups))
            return carry

        lax.fori_loop(1, groups, step, 0)

    def over_line(body):
        def step(s, carry):
            body(lax.rem(line + s, blocks))
            return carry

        lax.fori_loop(1, blocks, step, 0)

    def strips(x):
        x = x.reshape(planes, blocks, width, LANES)
        return jnp.swapaxes(x, 0, 1).reshape(blocks, piece, LANES)

    def level(t):
        return pl.ds(pl.multiple_of(t * piece, piece), piece)

    others = pl.ds(0, (blocks - 1) * piece)

    def wait_for(ref, sem):
        pltpu.make_async_copy(ref, ref, sem).wait()

    barrier = pltpu.get_barrier_semaphore()
    over_zone(lambda g: pl.semaphore_signal(barrier, inc=1, device_id={"zone": g}))
    over_line(lambda t: pl.semaphore_signal(barrier, inc=1, device_id={"line": t}))

    diagonal = iota((slots, slots), 0) == iota((slots, slots), 1)

    def column(row):
        return jnp.sum(jnp.where(diagonal, row, 0.0), axis=1, keepdims=True)

    for move in moves[:3]:
        move.wait()
    donor_row = donors[...].astype(f32)
    donor = column(donor_row)
    same_before = (donor == donor_row) & (iota((slots, slots), 1) < iota((slots, slots), 0))
    position = jnp.sum(jnp.where(same_before, 1.0, 0.0), axis=1, keepdims=True)
    lane = iota((slots, LANES), 1).astype(f32)
    line_pair = pairs[...].astype(f32)
    told = (
        jnp.where(lane == position, column(line_pair[0:1]), 0.0)
        + jnp.where(lane == position + capacity, column(line_pair[1:2]), 0.0)
        + jnp.where(lane == position + 2 * capacity, column(weights[...]), 0.0)
    )
    asks = jnp.where(iota((groups, slots), 0).astype(f32) == donor_row, 1.0, 0.0).astype(bf16)
    own_mixer = jnp.zeros((1, LANES), f32)
    for n in range(VARS * VARS):
        at = iota((1, LANES), 1) == 3 * capacity + n
        own_mixer = jnp.where(at, mixers[n, 0, 3], own_mixer)
    req_out[...] = (pick(asks, told) + own_mixer).reshape(groups, 1, LANES)
    moves[3].wait()

    def cut_state(v, carry):
        q_strips[v] = strips(q[v])
        return carry

    lax.fori_loop(0, VARS, cut_state, 0)

    pl.semaphore_wait(barrier, groups + blocks - 2)

    def send_request(g):
        pltpu.make_async_remote_copy(
            src_ref=req_out.at[g], dst_ref=req_in.at[zone],
            send_sem=req_sem.at[0], recv_sem=req_sem.at[1], device_id={"zone": g},
        ).start()

    over_zone(send_request)
    own_request = pltpu.make_async_copy(req_out.at[zone], req_in.at[zone], local_sem.at[0])
    own_request.start()

    def send_state(t):
        pltpu.make_async_remote_copy(
            src_ref=q_strips.at[:, t], dst_ref=q_turned.at[:, level(line)],
            send_sem=q_sem.at[0], recv_sem=q_sem.at[1], device_id={"line": t},
        ).start()

    over_line(send_state)
    own_state = pltpu.make_async_copy(
        q_strips.at[:, line], q_turned.at[:, level(line)], local_sem.at[1]
    )
    own_state.start()

    def part_state(v, carry):
        high, low = split(q[v].reshape(rows, LANES))
        q_both[v] = jnp.concatenate([high, low], 1)
        return carry

    lax.fori_loop(0, VARS, part_state, 0)

    own_request.wait()
    wait_for(req_in.at[pl.ds(0, groups - 1)], req_sem.at[1])
    asked = req_in[...].reshape(groups, LANES)
    cell_line = iota((groups, rows), 1).astype(f32)
    for n in range(capacity):
        share = asked[:, 2 * capacity + n:2 * capacity + n + 1]
        high, low = split(
            jnp.where(cell_line == asked[:, n:n + 1], share, 0.0)
            + jnp.where(cell_line == asked[:, capacity + n:capacity + n + 1], 1.0 - share, 0.0)
        )
        choose[n * groups:(n + 1) * groups] = high
        choose[named + n * groups:named + (n + 1) * groups] = low

    def interpolate(v, carry):
        both = dot(choose[...], q_both[v])
        lines[v] = (both[:named, :LANES] + both[:named, LANES:]) + both[named:, :LANES]
        return carry

    lax.fori_loop(0, VARS, interpolate, 0)

    def returned(g):
        return pl.ds(g * capacity, capacity)

    other_lines = pl.ds(0, named - capacity)
    own_lines = []
    for a in range(VARS):
        first = 3 * capacity + a * VARS
        scale = [
            jnp.broadcast_to(asked[:, first + v:first + v + 1], (groups, LANES)) for v in range(VARS)
        ]
        for n in range(capacity):
            at = slice(n * groups, (n + 1) * groups)
            total = scale[0] * lines[0, at]
            for v in range(1, VARS):
                total += scale[v] * lines[v, at]
            ret_out[a, :, n] = total.reshape(groups, 1, LANES)

        def send_lines(g):
            pltpu.make_async_remote_copy(
                src_ref=ret_out.at[a, g], dst_ref=ret_in.at[a, returned(zone)],
                send_sem=ret_send.at[a], recv_sem=ret_recv.at[a], device_id={"zone": g},
            ).start()

        over_zone(send_lines)
        copy = pltpu.make_async_copy(
            ret_out.at[a, zone], ret_in.at[a, returned(zone)], local_sem.at[2 + a]
        )
        copy.start()
        own_lines.append(copy)

    moves[4].wait()
    slot_of = donor * capacity + position
    here = jnp.sum(
        jnp.where(
            iota((slots, padded), 1).astype(f32) == slot_of,
            column(receivers[...].astype(f32)) + 1.0,
            0.0,
        ),
        axis=0,
        keepdims=True,
    ) - 1.0
    place[...] = jnp.where(iota((rows, padded), 0).astype(f32) == here, 1.0, 0.0).astype(bf16)
    is_receiver[...] = jnp.broadcast_to(
        jnp.sum(
            jnp.where(iota((rows, slots), 0) == receivers[...], 1.0, 0.0), axis=1, keepdims=True
        ),
        (rows, LANES),
    )
    if padded > named:
        ret_in[:, named:] = jnp.zeros((VARS, padded - named, 1, LANES), f32)

    moves[5].wait()
    first_columns = right_columns(deriv[0].T)
    second_rows = left_rows(deriv[1])

    def derive(v, carry):
        both = dot(q_both[v], first_columns)
        ddx[v] = both[:, :LANES] + both[:, LANES:]
        state = q_both[v]
        stacked = jnp.concatenate(
            [
                jnp.concatenate([state[k * edge:(k + 1) * edge, n:n + LANES] for k in range(planes)], 1)
                for n in (0, LANES)
            ],
            0,
        )
        both = dot(second_rows, stacked)
        both = both[:edge] + both[edge:]
        for k in range(planes):
            ddy[v, k * edge:(k + 1) * edge] = both[:, k * LANES:(k + 1) * LANES]
        return carry

    lax.fori_loop(0, VARS, derive, 0)
    tile = min(32, edge)

    def mix_of(m, a, x):
        total = mix(m, a, 0) * x[0]
        for v in range(1, VARS):
            total += mix(m, a, v) * x[v]
        return total

    def residual(n, carry):
        at = pl.ds(pl.multiple_of(n * tile, tile), tile)
        plane = n // (edge // tile)
        inside = pl.ds(pl.multiple_of(lax.rem(n, edge // tile) * tile, tile), tile)
        active = line * planes + plane < size[0]
        x = [ddx[v, at] for v in range(VARS)]
        y = [ddy[v, at] for v in range(VARS)]
        taken = is_receiver[at]
        r = [
            jnp.where(active, -(mix_of(0, a, x) + mix_of(1, a, y)), 0.0) - taken * q[a, plane, inside]
            for a in range(VARS)
        ]
        for a in range(VARS):
            part[a, at] = mix_of(3, a, r)
        return carry

    lax.fori_loop(0, rows // tile, residual, 0)

    moves[6].wait()
    own_state.wait()
    wait_for(q_turned.at[:, others], q_sem.at[1])

    def whole_lines(ref, v):
        return jnp.concatenate(
            [ref[v, pl.ds(j, depth, stride=width), :] for j in range(width)], 1
        )

    def derive_z(v, carry):
        zed[v] = left_mul(deriv_z[...], whole_lines(q_turned, v))
        return carry

    lax.fori_loop(0, VARS, derive_z, 0)
    levels = min(32, depth)

    def residual_z(n, carry):
        deep = lax.rem(n, depth // levels) * levels
        down = pl.ds(pl.multiple_of(deep, levels), levels)
        at = pl.ds(pl.multiple_of(n // (depth // levels) * LANES, LANES), LANES)
        active = iota((levels, LANES), 0) + deep < size[0]
        z = [zed[v, down, at] for v in range(VARS)]
        r = [jnp.where(active, -mix_of(2, a, z), 0.0) for a in range(VARS)]
        for a in range(VARS):
            mixed[a, down, at] = mix_of(3, a, r)
        return carry

    lax.fori_loop(0, width * (depth // levels), residual_z, 0)
    moves[7].wait()

    def add_source(a):
        wait_for(ret_in.at[a, other_lines], ret_recv.at[a])
        high, low = split(ret_in[a].reshape(padded, LANES))
        both = dot(place[...], jnp.concatenate([high, low], 1))
        part_strips[a] = strips(part[a] + (both[:, :LANES] + both[:, LANES:]))

        def send_part(t):
            pltpu.make_async_remote_copy(
                src_ref=part_strips.at[a, t], dst_ref=part_turned.at[a, level(line)],
                send_sem=part_send.at[a], recv_sem=part_recv.at[a], device_id={"line": t},
            ).start()

        over_line(send_part)
        part_turned[a, level(line)] = part_strips[a, line]

    def solve_z(a):
        wait_for(part_turned.at[a, others], part_recv.at[a])
        solved = left_mul(inverse_z[a], whole_lines(part_turned, a) + mixed[a])
        for j in range(width):
            turned_back[a, pl.ds(j, depth, stride=width), :] = solved[:, j * LANES:(j + 1) * LANES]

        def send_back(t):
            pltpu.make_async_remote_copy(
                src_ref=turned_back.at[a, level(t)], dst_ref=back.at[a, line],
                send_sem=back_send.at[a], recv_sem=back_recv.at[a], device_id={"line": t},
            ).start()

        over_line(send_back)
        back[a, line] = turned_back[a, level(line)]

    for copy in own_lines:
        copy.wait()
    add_source(0)

    def source_and_solve(a, carry):
        add_source(a)
        solve_z(a - 1)
        return carry

    lax.fori_loop(1, VARS, source_and_solve, 0)
    solve_z(VARS - 1)

    moves[8].wait()
    for a in range(VARS - 1):
        wait_for(turned_back.at[a, others], back_recv.at[a])
    last = VARS - 1
    strip_tile = min(4, blocks)

    def all_but_last(n, carry):
        at = pl.ds(n * strip_tile, strip_tile)
        x = [back[a, at] for a in range(last)]
        for v in range(VARS):
            total = mix(4, v, 0) * x[0]
            for a in range(1, last):
                total += mix(4, v, a) * x[a]
            step_b[v, at] = total
        return carry

    lax.fori_loop(0, blocks // strip_tile, all_but_last, 0)
    wait_for(turned_back.at[last, others], back_recv.at[last])

    def solve_y(v, carry):
        x = step_b[v] + mixers[v * VARS + last, 0, 4] * back[last]
        x = jnp.concatenate(
            [x[:, k * width:(k + 1) * width, :].reshape(edge, LANES) for k in range(planes)], 1
        )
        both = left_mul(inverse[1, v], x)
        for k in range(planes):
            step_a[v, k * edge:(k + 1) * edge] = both[:, k * LANES:(k + 1) * LANES]
        return carry

    lax.fori_loop(0, VARS, solve_y, 0)

    def mix_second(n, carry):
        at = pl.ds(pl.multiple_of(n * tile, tile), tile)
        x = [step_a[v, at] for v in range(VARS)]
        for a in range(VARS):
            ddx[a, at] = mix_of(5, a, x)
        return carry

    lax.fori_loop(0, rows // tile, mix_second, 0)

    def solve_x(v, carry):
        ddy[v] = right_mul(ddx[v], right_columns(inverse[0, v].T))
        return carry

    lax.fori_loop(0, VARS, solve_x, 0)

    def mix_last(n, carry):
        at = pl.ds(pl.multiple_of(n * tile, tile), tile)
        inside = pl.ds(pl.multiple_of(lax.rem(n, edge // tile) * tile, tile), tile)
        x = [ddy[v, at] for v in range(VARS)]
        for a in range(VARS):
            out[a, n // (edge // tile), inside] = mix_of(6, a, x)
        return carry

    lax.fori_loop(0, rows // tile, mix_last, 0)

    wait_for(req_in.at[pl.ds(0, groups - 1)], req_sem.at[0])
    wait_for(q_turned.at[:, others], q_sem.at[0])
    for a in range(VARS):
        wait_for(ret_in.at[a, other_lines], ret_send.at[a])
        wait_for(part_turned.at[a, others], part_send.at[a])
        wait_for(turned_back.at[a, others], back_send.at[a])


def local(
    flow_state, derivative, derivative_z, line_inverse, line_inverse_z, mixers, zone_size,
    receiver_line, donor_group, donor_line, stencil_weight,
):
    groups, blocks = lax.axis_size("zone"), lax.axis_size("line")
    planes, edge = flow_state.shape[2], flow_state.shape[3]
    slots = receiver_line.shape[2]
    capacity = max(2, 5 * slots // (2 * groups))
    rows, depth, width = planes * edge, planes * blocks, edge // blocks
    named = groups * capacity
    padded = -(-named // LANES) * LANES
    dma = pltpu.SemaphoreType.DMA
    vmem = pl.BlockSpec(memory_space=pltpu.VMEM)
    hbm = pl.BlockSpec(memory_space=pltpu.HBM)
    smem = pl.BlockSpec(memory_space=pltpu.SMEM)
    result = pl.pallas_call(
        functools.partial(kernel, capacity),
        out_shape=jax.ShapeDtypeStruct((VARS, planes, edge, LANES), f32),
        in_specs=[hbm] * 5 + [smem] * 2 + [hbm] * 4,
        out_specs=vmem,
        scratch_shapes=[
            pltpu.VMEM((VARS, planes, edge, LANES), f32),
            pltpu.VMEM(derivative.shape, f32),
            pltpu.VMEM(derivative_z.shape, f32),
            pltpu.VMEM(line_inverse.shape[1:], f32),
            pltpu.VMEM(line_inverse_z.shape[1:], f32),
            pltpu.VMEM((1, slots), jnp.int32),
            pltpu.VMEM((1, slots), jnp.int32),
            pltpu.VMEM((2, slots), jnp.int32),
            pltpu.VMEM((1, slots), f32),
            pltpu.VMEM((groups, 1, LANES), f32),
            pltpu.VMEM((groups, 1, LANES), f32),
            pltpu.VMEM((VARS, blocks, planes * width, LANES), f32),
            pltpu.VMEM((VARS, rows, 2 * LANES), bf16),
            pltpu.VMEM((VARS, depth * width, LANES), f32),
            pltpu.VMEM((VARS, rows, LANES), f32),
            pltpu.VMEM((VARS, rows, LANES), f32),
            pltpu.VMEM((VARS, rows, LANES), f32),
            pltpu.VMEM((VARS, blocks, planes * width, LANES), f32),
            pltpu.VMEM((rows, LANES), f32),
            pltpu.VMEM((VARS, named, LANES), f32),
            pltpu.VMEM((VARS, groups, capacity, 1, LANES), f32),
            pltpu.VMEM((VARS, padded, 1, LANES), f32),
            pltpu.VMEM((2 * named, rows), bf16),
            pltpu.VMEM((rows, padded), bf16),
            pltpu.VMEM((VARS, depth * width, LANES), f32),
            pltpu.VMEM((VARS, depth, width * LANES), f32),
            pltpu.VMEM((VARS, depth, width * LANES), f32),
            pltpu.VMEM((VARS, depth * width, LANES), f32),
            pltpu.VMEM((VARS, blocks, planes * width, LANES), f32),
            pltpu.VMEM((VARS, rows, LANES), f32),
            pltpu.VMEM((VARS, blocks, planes * width, LANES), f32),
            dma((9,)),
            dma((2 + VARS,)),
            dma((2,)),
            dma((2,)),
        ] + [dma((VARS,))] * 6,
        compiler_params=pltpu.CompilerParams(
            collective_id=0, has_side_effects=True, vmem_limit_bytes=48 * 2**20
        ),
    )(
        flow_state[0], derivative, derivative_z, line_inverse[0], line_inverse_z[0],
        jnp.transpose(mixers[0], (1, 2, 0)).reshape(VARS * VARS, 1, mixers.shape[1]),
        zone_size, receiver_line[0], donor_group[0, :, :, 0], donor_line[0, 0].T,
        stencil_weight[0],
    )
    return result[None]


def solution(mesh):
    placed = (
        P("zone", None, "line", None, None),
        P(),
        P(),
        P("zone", None, None, None, None),
        P("zone", None, None, None),
        P("zone", None, None, None),
        P("zone"),
        P("zone", "line", None),
        P("zone", "line", None, None),
        P("zone", "line", None, None),
        P("zone", "line", None),
    )
    return jax.shard_map(
        local,
        mesh=mesh,
        in_specs=placed,
        out_specs=P("zone", None, "line", None, None),
        check_vma=False,
    )
```

```python
import functools

import jax
import jax.numpy as jnp
from jax import lax
from jax.experimental import pallas as pl
from jax.experimental.pallas import tpu as pltpu
from jax.sharding import PartitionSpec as P

f32 = jnp.float32
bf16 = jnp.bfloat16
VARS = 5
LANES = 128


def split(x):
    high = x.astype(bf16)
    return high, (x - high.astype(f32)).astype(bf16)


def dot(a, b):
    return jnp.dot(a, b, preferred_element_type=f32)


def left_rows(w):
    high, low = split(w)
    return jnp.concatenate(
        [jnp.concatenate([high, high], 1), jnp.concatenate([low, jnp.zeros_like(low)], 1)], 0
    )


def left_mul(rows, x):
    high, low = split(x)
    both = dot(rows, jnp.concatenate([high, low], 0))
    half = x.shape[0]
    return both[:half] + both[half:]


def right_columns(w):
    high, low = split(w)
    return jnp.concatenate(
        [jnp.concatenate([high, low], 1), jnp.concatenate([high, jnp.zeros_like(low)], 1)], 0
    )


def right_mul(x, columns):
    high, low = split(x)
    both = dot(jnp.concatenate([high, low], 1), columns)
    half = columns.shape[1] // 2
    return both[:, :half] + both[:, half:]


def pick(rows, x):
    first, rest = split(x)
    rest = x - first.astype(f32)
    second = rest.astype(bf16)
    third = (rest - second.astype(f32)).astype(bf16)
    return (dot(rows, first) + dot(rows, second)) + dot(rows, third)


def iota(shape, axis):
    return lax.broadcasted_iota(jnp.int32, shape, axis)


def kernel(
    capacity,
    q_hbm, deriv_hbm, deriv_z_hbm, inverse_hbm, inverse_z_hbm, mixers, size,
    receivers_hbm, donors_hbm, pairs_hbm, weights_hbm,
    out,
    q, deriv, deriv_z, inverse, inverse_z, receivers, donors, pairs, weights,
    req_out, req_in, q_strips, q_both, q_turned, ddx, ddy, part, part_strips, is_receiver,
    lines, ret_out, ret_in, choose, place, rows_z, rows_y, columns_x,
    part_turned, zed, mixed, turned_back, back, step_a, step_b,
    load_sem, local_sem, req_sem, q_sem,
    ret_send, ret_recv, part_send, part_recv, back_send, back_recv,
):
    groups, blocks = lax.axis_size("zone"), lax.axis_size("line")
    zone, line = lax.axis_index("zone"), lax.axis_index("line")

    def mix(m, a, v):
        return mixers[a * VARS + v, 0, m]

    moves = [
        pltpu.make_async_copy(source, target, load_sem.at[n])
        for n, (source, target) in enumerate((
            (donors_hbm, donors), (pairs_hbm, pairs), (weights_hbm, weights), (q_hbm, q),
            (receivers_hbm, receivers), (deriv_hbm, deriv), (deriv_z_hbm, deriv_z),
            (inverse_z_hbm, inverse_z), (inverse_hbm, inverse),
        ))
    ]
    for move in moves:
        move.start()
    planes, edge = q.shape[1], q.shape[2]
    rows = planes * edge
    depth = planes * blocks
    width = edge // blocks
    slots = receivers.shape[1]
    piece = planes * width
    named = groups * capacity
    padded = ret_in.shape[1]

    def over_zone(body):
        def step(s, carry):
            body(lax.rem(zone + s, groups))
            return carry

        lax.fori_loop(1, groups, step, 0)

    def over_line(body):
        def step(s, carry):
            body(lax.rem(line + s, blocks))
            return carry

        lax.fori_loop(1, blocks, step, 0)

    def strips(x):
        x = x.reshape(planes, blocks, width, LANES)
        return jnp.swapaxes(x, 0, 1).reshape(blocks, piece, LANES)

    def level(t):
        return pl.ds(pl.multiple_of(t * piece, piece), piece)

    others = pl.ds(0, (blocks - 1) * piece)

    def wait_for(ref, sem):
        pltpu.make_async_copy(ref, ref, sem).wait()

    barrier = pltpu.get_barrier_semaphore()
    over_zone(lambda g: pl.semaphore_signal(barrier, inc=1, device_id={"zone": g}))
    over_line(lambda t: pl.semaphore_signal(barrier, inc=1, device_id={"line": t}))

    diagonal = iota((slots, slots), 0) == iota((slots, slots), 1)

    def column(row):
        return jnp.sum(jnp.where(diagonal, row, 0.0), axis=1, keepdims=True)

    for move in moves[:3]:
        move.wait()
    donor_row = donors[...].astype(f32)
    donor = column(donor_row)
    same_before = (donor == donor_row) & (iota((slots, slots), 1) < iota((slots, slots), 0))
    position = jnp.sum(jnp.where(same_before, 1.0, 0.0), axis=1, keepdims=True)
    lane = iota((slots, LANES), 1).astype(f32)
    line_pair = pairs[...].astype(f32)
    told = (
        jnp.where(lane == position, column(line_pair[0:1]), 0.0)
        + jnp.where(lane == position + capacity, column(line_pair[1:2]), 0.0)
        + jnp.where(lane == position + 2 * capacity, column(weights[...]), 0.0)
    )
    asks = jnp.where(iota((groups, slots), 0).astype(f32) == donor_row, 1.0, 0.0).astype(bf16)
    own_mixer = jnp.zeros((1, LANES), f32)
    for n in range(VARS * VARS):
        at = iota((1, LANES), 1) == 3 * capacity + n
        own_mixer = jnp.where(at, mixers[n, 0, 3], own_mixer)
    req_out[...] = (pick(asks, told) + own_mixer).reshape(groups, 1, LANES)
    moves[3].wait()

    def cut_state(v, carry):
        q_strips[v] = strips(q[v])
        return carry

    lax.fori_loop(0, VARS, cut_state, 0)

    pl.semaphore_wait(barrier, groups + blocks - 2)

    def send_request(g):
        pltpu.make_async_remote_copy(
            src_ref=req_out.at[g], dst_ref=req_in.at[zone],
            send_sem=req_sem.at[0], recv_sem=req_sem.at[1], device_id={"zone": g},
        ).start()

    over_zone(send_request)
    own_request = pltpu.make_async_copy(req_out.at[zone], req_in.at[zone], local_sem.at[0])
    own_request.start()

    def send_state(t):
        pltpu.make_async_remote_copy(
            src_ref=q_strips.at[:, t], dst_ref=q_turned.at[:, level(line)],
            send_sem=q_sem.at[0], recv_sem=q_sem.at[1], device_id={"line": t},
        ).start()

    over_line(send_state)
    own_state = pltpu.make_async_copy(
        q_strips.at[:, line], q_turned.at[:, level(line)], local_sem.at[1]
    )
    own_state.start()

    def part_state(v, carry):
        high, low = split(q[v].reshape(rows, LANES))
        q_both[v] = jnp.concatenate([high, low], 1)
        return carry

    lax.fori_loop(0, VARS, part_state, 0)

    own_request.wait()
    wait_for(req_in.at[pl.ds(0, groups - 1)], req_sem.at[1])
    asked = req_in[...].reshape(groups, LANES)
    cell_line = iota((groups, rows), 1).astype(f32)
    for n in range(capacity):
        share = asked[:, 2 * capacity + n:2 * capacity + n + 1]
        high, low = split(
            jnp.where(cell_line == asked[:, n:n + 1], share, 0.0)
            + jnp.where(cell_line == asked[:, capacity + n:capacity + n + 1], 1.0 - share, 0.0)
        )
        choose[n * groups:(n + 1) * groups] = high
        choose[named + n * groups:named + (n + 1) * groups] = low

    def interpolate(v, carry):
        both = dot(choose[...], q_both[v])
        lines[v] = (both[:named, :LANES] + both[:named, LANES:]) + both[named:, :LANES]
        return carry

    lax.fori_loop(0, VARS, interpolate, 0, unroll=True)

    def returned(g):
        return pl.ds(g * capacity, capacity)

    other_lines = pl.ds(0, named - capacity)
    own_lines = []

    def send_lines(a):
        def send(g):
            pltpu.make_async_remote_copy(
                src_ref=ret_out.at[a, g], dst_ref=ret_in.at[a, returned(zone)],
                send_sem=ret_send.at[a], recv_sem=ret_recv.at[a], device_id={"zone": g},
            ).start()

        over_zone(send)

    for a in range(VARS):
        first = 3 * capacity + a * VARS
        scale = [
            jnp.broadcast_to(asked[:, first + v:first + v + 1], (groups, LANES)) for v in range(VARS)
        ]
        for n in range(capacity):
            at = slice(n * groups, (n + 1) * groups)
            total = scale[0] * lines[0, at]
            for v in range(1, VARS):
                total += scale[v] * lines[v, at]
            ret_out[a, :, n] = total.reshape(groups, 1, LANES)

        send_lines(a)
        copy = pltpu.make_async_copy(
            ret_out.at[a, zone], ret_in.at[a, returned(zone)], local_sem.at[2 + a]
        )
        copy.start()
        own_lines.append(copy)

    moves[4].wait()
    slot_of = donor * capacity + position
    here = jnp.sum(
        jnp.where(
            iota((slots, padded), 1).astype(f32) == slot_of,
            column(receivers[...].astype(f32)) + 1.0,
            0.0,
        ),
        axis=0,
        keepdims=True,
    ) - 1.0
    place[...] = jnp.where(iota((rows, padded), 0).astype(f32) == here, 1.0, 0.0).astype(bf16)
    is_receiver[...] = jnp.broadcast_to(
        jnp.sum(
            jnp.where(iota((rows, slots), 0) == receivers[...], 1.0, 0.0), axis=1, keepdims=True
        ),
        (rows, LANES),
    )
    if padded > named:
        ret_in[:, named:] = jnp.zeros((VARS, padded - named, 1, LANES), f32)

    moves[5].wait()
    first_columns = right_columns(deriv[0].T)
    second_rows = left_rows(deriv[1])

    def derive(v, carry):
        both = dot(q_both[v], first_columns)
        ddx[v] = both[:, :LANES] + both[:, LANES:]
        state = q_both[v]
        stacked = jnp.concatenate(
            [
                jnp.concatenate([state[k * edge:(k + 1) * edge, n:n + LANES] for k in range(planes)], 1)
                for n in (0, LANES)
            ],
            0,
        )
        both = dot(second_rows, stacked)
        both = both[:edge] + both[edge:]
        for k in range(planes):
            ddy[v, k * edge:(k + 1) * edge] = both[:, k * LANES:(k + 1) * LANES]
        return carry

    lax.fori_loop(0, VARS, derive, 0)
    tile = min(32, edge)

    def mix_of(m, a, x):
        total = mix(m, a, 0) * x[0]
        for v in range(1, VARS):
            total += mix(m, a, v) * x[v]
        return total

    def residual(n, carry):
        at = pl.ds(pl.multiple_of(n * tile, tile), tile)
        plane = n // (edge // tile)
        inside = pl.ds(pl.multiple_of(lax.rem(n, edge // tile) * tile, tile), tile)
        active = line * planes + plane < size[0]
        x = [ddx[v, at] for v in range(VARS)]
        y = [ddy[v, at] for v in range(VARS)]
        taken = is_receiver[at]
        r = [
            jnp.where(active, -(mix_of(0, a, x) + mix_of(1, a, y)), 0.0) - taken * q[a, plane, inside]
            for a in range(VARS)
        ]
        for a in range(VARS):
            part[a, at] = mix_of(3, a, r)
        return carry

    lax.fori_loop(0, rows // tile, residual, 0)

    moves[6].wait()
    own_state.wait()
    wait_for(q_turned.at[:, others], q_sem.at[1])

    def whole_lines(ref, v):
        return jnp.concatenate(
            [ref[v, pl.ds(j, depth, stride=width), :] for j in range(width)], 1
        )

    third_rows = left_rows(deriv_z[...])

    def derive_z(v, carry):
        zed[v] = left_mul(third_rows, whole_lines(q_turned, v))
        return carry

    lax.fori_loop(0, VARS, derive_z, 0)
    levels = min(32, depth)

    def residual_z(n, carry):
        deep = lax.rem(n, depth // levels) * levels
        down = pl.ds(pl.multiple_of(deep, levels), levels)
        at = pl.ds(pl.multiple_of(n // (depth // levels) * LANES, LANES), LANES)
        active = iota((levels, LANES), 0) + deep < size[0]
        z = [zed[v, down, at] for v in range(VARS)]
        r = [jnp.where(active, -mix_of(2, a, z), 0.0) for a in range(VARS)]
        for a in range(VARS):
            mixed[a, down, at] = mix_of(3, a, r)
        return carry

    lax.fori_loop(0, width * (depth // levels), residual_z, 0)
    moves[7].wait()
    moves[8].wait()

    def prepare(v, carry):
        rows_z[v] = left_rows(inverse_z[v])
        rows_y[v] = left_rows(inverse[1, v])
        columns_x[v] = right_columns(inverse[0, v].T)
        return carry

    lax.fori_loop(0, VARS, prepare, 0)

    def add_source(a):
        wait_for(ret_in.at[a, other_lines], ret_recv.at[a])
        high, low = split(ret_in[a].reshape(padded, LANES))
        both = dot(place[...], jnp.concatenate([high, low], 1))
        part_strips[a] = strips(part[a] + (both[:, :LANES] + both[:, LANES:]))

        def send_part(t):
            pltpu.make_async_remote_copy(
                src_ref=part_strips.at[a, t], dst_ref=part_turned.at[a, level(line)],
                send_sem=part_send.at[a], recv_sem=part_recv.at[a], device_id={"line": t},
            ).start()

        over_line(send_part)
        part_turned[a, level(line)] = part_strips[a, line]

    def solve_z(a):
        wait_for(part_turned.at[a, others], part_recv.at[a])
        solved = left_mul(rows_z[a], whole_lines(part_turned, a) + mixed[a])
        for j in range(width):
            turned_back[a, pl.ds(j, depth, stride=width), :] = solved[:, j * LANES:(j + 1) * LANES]

        def send_back(t):
            pltpu.make_async_remote_copy(
                src_ref=turned_back.at[a, level(t)], dst_ref=back.at[a, line],
                send_sem=back_send.at[a], recv_sem=back_recv.at[a], device_id={"line": t},
            ).start()

        over_line(send_back)
        back[a, line] = turned_back[a, level(line)]

    for copy in own_lines:
        copy.wait()
    add_source(0)

    def source_and_solve(a, carry):
        add_source(a)
        solve_z(a - 1)
        return carry

    lax.fori_loop(1, VARS, source_and_solve, 0)
    solve_z(VARS - 1)

    for a in range(VARS - 1):
        wait_for(turned_back.at[a, others], back_recv.at[a])
    last = VARS - 1
    strip_tile = min(4, blocks)

    def all_but_last(n, carry):
        at = pl.ds(n * strip_tile, strip_tile)
        x = [back[a, at] for a in range(last)]
        for v in range(VARS):
            total = mix(4, v, 0) * x[0]
            for a in range(1, last):
                total += mix(4, v, a) * x[a]
            step_b[v, at] = total
        return carry

    lax.fori_loop(0, blocks // strip_tile, all_but_last, 0)
    wait_for(turned_back.at[last, others], back_recv.at[last])

    def solve_y(v, carry):
        x = step_b[v] + mixers[v * VARS + last, 0, 4] * back[last]
        x = jnp.concatenate(
            [x[:, k * width:(k + 1) * width, :].reshape(edge, LANES) for k in range(planes)], 1
        )
        both = left_mul(rows_y[v], x)
        for k in range(planes):
            step_a[v, k * edge:(k + 1) * edge] = both[:, k * LANES:(k + 1) * LANES]
        return carry

    lax.fori_loop(0, VARS, solve_y, 0, unroll=True)

    def mix_second(n, carry):
        at = pl.ds(pl.multiple_of(n * tile, tile), tile)
        x = [step_a[v, at] for v in range(VARS)]
        for a in range(VARS):
            ddx[a, at] = mix_of(5, a, x)
        return carry

    lax.fori_loop(0, rows // tile, mix_second, 0)

    def solve_x(v, carry):
        ddy[v] = right_mul(ddx[v], columns_x[v])
        return carry

    lax.fori_loop(0, VARS, solve_x, 0, unroll=True)

    def mix_last(n, carry):
        at = pl.ds(pl.multiple_of(n * tile, tile), tile)
        inside = pl.ds(pl.multiple_of(lax.rem(n, edge // tile) * tile, tile), tile)
        x = [ddy[v, at] for v in range(VARS)]
        for a in range(VARS):
            out[a, n // (edge // tile), inside] = mix_of(6, a, x)
        return carry

    lax.fori_loop(0, rows // tile, mix_last, 0)

    wait_for(req_in.at[pl.ds(0, groups - 1)], req_sem.at[0])
    wait_for(q_turned.at[:, others], q_sem.at[0])
    for a in range(VARS):
        wait_for(ret_in.at[a, other_lines], ret_send.at[a])
        wait_for(part_turned.at[a, others], part_send.at[a])
        wait_for(turned_back.at[a, others], back_send.at[a])


def local(
    flow_state, derivative, derivative_z, line_inverse, line_inverse_z, mixers, zone_size,
    receiver_line, donor_group, donor_line, stencil_weight,
):
    groups, blocks = lax.axis_size("zone"), lax.axis_size("line")
    planes, edge = flow_state.shape[2], flow_state.shape[3]
    slots = receiver_line.shape[2]
    capacity = max(2, 5 * slots // (2 * groups))
    rows, depth, width = planes * edge, planes * blocks, edge // blocks
    named = groups * capacity
    padded = -(-named // LANES) * LANES
    dma = pltpu.SemaphoreType.DMA
    vmem = pl.BlockSpec(memory_space=pltpu.VMEM)
    hbm = pl.BlockSpec(memory_space=pltpu.HBM)
    smem = pl.BlockSpec(memory_space=pltpu.SMEM)
    result = pl.pallas_call(
        functools.partial(kernel, capacity),
        out_shape=jax.ShapeDtypeStruct((VARS, planes, edge, LANES), f32),
        in_specs=[hbm] * 5 + [smem] * 2 + [hbm] * 4,
        out_specs=vmem,
        scratch_shapes=[
            pltpu.VMEM((VARS, planes, edge, LANES), f32),
            pltpu.VMEM(derivative.shape, f32),
            pltpu.VMEM(derivative_z.shape, f32),
            pltpu.VMEM(line_inverse.shape[1:], f32),
            pltpu.VMEM(line_inverse_z.shape[1:], f32),
            pltpu.VMEM((1, slots), jnp.int32),
            pltpu.VMEM((1, slots), jnp.int32),
            pltpu.VMEM((2, slots), jnp.int32),
            pltpu.VMEM((1, slots), f32),
            pltpu.VMEM((groups, 1, LANES), f32),
            pltpu.VMEM((groups, 1, LANES), f32),
            pltpu.VMEM((VARS, blocks, planes * width, LANES), f32),
            pltpu.VMEM((VARS, rows, 2 * LANES), bf16),
            pltpu.VMEM((VARS, depth * width, LANES), f32),
            pltpu.VMEM((VARS, rows, LANES), f32),
            pltpu.VMEM((VARS, rows, LANES), f32),
            pltpu.VMEM((VARS, rows, LANES), f32),
            pltpu.VMEM((VARS, blocks, planes * width, LANES), f32),
            pltpu.VMEM((rows, LANES), f32),
            pltpu.VMEM((VARS, named, LANES), f32),
            pltpu.VMEM((VARS, groups, capacity, 1, LANES), f32),
            pltpu.VMEM((VARS, padded, 1, LANES), f32),
            pltpu.VMEM((2 * named, rows), bf16),
            pltpu.VMEM((rows, padded), bf16),
            pltpu.VMEM((VARS, 2 * depth, 2 * depth), bf16),
            pltpu.VMEM((VARS, 2 * edge, 2 * edge), bf16),
            pltpu.VMEM((VARS, 2 * LANES, 2 * LANES), bf16),
            pltpu.VMEM((VARS, depth * width, LANES), f32),
            pltpu.VMEM((VARS, depth, width * LANES), f32),
            pltpu.VMEM((VARS, depth, width * LANES), f32),
            pltpu.VMEM((VARS, depth * width, LANES), f32),
            pltpu.VMEM((VARS, blocks, planes * width, LANES), f32),
            pltpu.VMEM((VARS, rows, LANES), f32),
            pltpu.VMEM((VARS, blocks, planes * width, LANES), f32),
            dma((9,)),
            dma((2 + VARS,)),
            dma((2,)),
            dma((2,)),
        ] + [dma((VARS,))] * 6,
        compiler_params=pltpu.CompilerParams(
            collective_id=0, has_side_effects=True, vmem_limit_bytes=56 * 2**20
        ),
    )(
        flow_state[0], derivative, derivative_z, line_inverse[0], line_inverse_z[0],
        jnp.transpose(mixers[0], (1, 2, 0)).reshape(VARS * VARS, 1, mixers.shape[1]),
        zone_size, receiver_line[0], donor_group[0, :, :, 0], donor_line[0, 0].T,
        stencil_weight[0],
    )
    return result[None]


def solution(mesh):
    placed = (
        P("zone", None, "line", None, None),
        P(),
        P(),
        P("zone", None, None, None, None),
        P("zone", None, None, None),
        P("zone", None, None, None),
        P("zone"),
        P("zone", "line", None),
        P("zone", "line", None, None),
        P("zone", "line", None, None),
        P("zone", "line", None),
    )
    return jax.shard_map(
        local,
        mesh=mesh,
        in_specs=placed,
        out_specs=P("zone", None, "line", None, None),
        check_vma=False,
    )
```

```python
import functools

import jax
import jax.numpy as jnp
from jax import lax
from jax.experimental import pallas as pl
from jax.experimental.pallas import tpu as pltpu
from jax.sharding import PartitionSpec as P

f32 = jnp.float32
bf16 = jnp.bfloat16
VARS = 5
LANES = 128


def split(x):
    high = x.astype(bf16)
    return high, (x - high.astype(f32)).astype(bf16)


def dot(a, b):
    return jnp.dot(a, b, preferred_element_type=f32)


def left_rows(w):
    high, low = split(w)
    return jnp.concatenate(
        [jnp.concatenate([high, high], 1), jnp.concatenate([low, jnp.zeros_like(low)], 1)], 0
    )


def left_mul(rows, x):
    high, low = split(x)
    both = dot(rows, jnp.concatenate([high, low], 0))
    half = x.shape[0]
    return both[:half] + both[half:]


def right_columns(w):
    high, low = split(w)
    return jnp.concatenate(
        [jnp.concatenate([high, low], 1), jnp.concatenate([high, jnp.zeros_like(low)], 1)], 0
    )


def right_mul(x, columns):
    high, low = split(x)
    both = dot(jnp.concatenate([high, low], 1), columns)
    half = columns.shape[1] // 2
    return both[:, :half] + both[:, half:]


def pick(rows, x):
    first, rest = split(x)
    rest = x - first.astype(f32)
    second = rest.astype(bf16)
    third = (rest - second.astype(f32)).astype(bf16)
    return (dot(rows, first) + dot(rows, second)) + dot(rows, third)


def iota(shape, axis):
    return lax.broadcasted_iota(jnp.int32, shape, axis)


def kernel(
    capacity,
    q_hbm, deriv_hbm, deriv_z_hbm, inverse_hbm, inverse_z_hbm, mixers, size,
    receivers_hbm, donors_hbm, pairs_hbm, weights_hbm,
    out,
    q, deriv, deriv_z, inverse, inverse_z, receivers, donors, pairs, weights,
    req_out, req_in, told_all, q_strips, q_both, q_turned, ddx, ddy, part, part_strips, is_receiver,
    lines, ret_out, ret_in, choose, place, rows_z, rows_y, columns_x,
    part_turned, zed, mixed, turned_back, back, step_a, step_b,
    load_sem, local_sem, req_sem, q_sem,
    ret_send, ret_recv, part_send, part_recv, back_send, back_recv,
):
    groups, blocks = lax.axis_size("zone"), lax.axis_size("line")
    zone, line = lax.axis_index("zone"), lax.axis_index("line")

    def mix(m, a, v):
        return mixers[a, v, m]

    moves = [
        pltpu.make_async_copy(source, target, load_sem.at[n])
        for n, (source, target) in enumerate((
            (donors_hbm, donors), (pairs_hbm, pairs), (weights_hbm, weights), (q_hbm, q),
            (receivers_hbm, receivers), (deriv_hbm, deriv), (deriv_z_hbm, deriv_z),
            (inverse_z_hbm, inverse_z), (inverse_hbm, inverse),
        ))
    ]
    for move in moves:
        move.start()
    planes, edge = q.shape[1], q.shape[2]
    rows = planes * edge
    depth = planes * blocks
    width = edge // blocks
    slots = receivers.shape[1]
    piece = planes * width
    named = groups * capacity
    padded = ret_in.shape[1]

    def over_zone(body):
        def step(s, carry):
            body(lax.rem(zone + s, groups))
            return carry

        lax.fori_loop(1, groups, step, 0)

    def over_line(body):
        def step(s, carry):
            body(lax.rem(line + s, blocks))
            return carry

        lax.fori_loop(1, blocks, step, 0)

    def strips(x):
        x = x.reshape(planes, blocks, width, LANES)
        return jnp.swapaxes(x, 0, 1).reshape(blocks, piece, LANES)

    def level(t):
        return pl.ds(pl.multiple_of(t * piece, piece), piece)

    others = pl.ds(0, (blocks - 1) * piece)

    def wait_for(ref, sem):
        pltpu.make_async_copy(ref, ref, sem).wait()

    barrier = pltpu.get_barrier_semaphore()
    over_zone(lambda g: pl.semaphore_signal(barrier, inc=1, device_id={"zone": g}))
    over_line(lambda t: pl.semaphore_signal(barrier, inc=1, device_id={"line": t}))

    diagonal = iota((slots, slots), 0) == iota((slots, slots), 1)

    def column(row):
        return jnp.sum(jnp.where(diagonal, row, 0.0), axis=1, keepdims=True)

    for move in moves[:3]:
        move.wait()
    donor_row = donors[...].astype(f32)
    donor = column(donor_row)
    same_before = (donor == donor_row) & (iota((slots, slots), 1) < iota((slots, slots), 0))
    position = jnp.sum(jnp.where(same_before, 1.0, 0.0), axis=1, keepdims=True)
    lane = iota((slots, LANES), 1).astype(f32)
    line_pair = pairs[...].astype(f32)
    told = (
        jnp.where(lane == position, column(line_pair[0:1]), 0.0)
        + jnp.where(lane == position + capacity, column(line_pair[1:2]), 0.0)
        + jnp.where(lane == position + 2 * capacity, column(weights[...]), 0.0)
    )
    asks = jnp.where(iota((groups, slots), 0).astype(f32) == donor_row, 1.0, 0.0).astype(bf16)
    own_mixer = jnp.zeros((1, LANES), f32)
    for n in range(VARS * VARS):
        at = iota((1, LANES), 1) == 3 * capacity + n
        own_mixer = jnp.where(at, mixers[n // VARS, n % VARS, 3], own_mixer)
    req_out[...] = (pick(asks, told) + own_mixer).reshape(groups, 1, LANES)
    moves[3].wait()

    def cut_state(v, carry):
        q_strips[v] = strips(q[v])
        return carry

    lax.fori_loop(0, VARS, cut_state, 0)

    pl.semaphore_wait(barrier, groups + blocks - 2)

    def send_request(g):
        pltpu.make_async_remote_copy(
            src_ref=req_out.at[g], dst_ref=req_in.at[zone],
            send_sem=req_sem.at[0], recv_sem=req_sem.at[1], device_id={"zone": g},
        ).start()

    over_zone(send_request)
    own_request = pltpu.make_async_copy(req_out.at[zone], req_in.at[zone], local_sem.at[0])
    own_request.start()

    def send_state(t):
        pltpu.make_async_remote_copy(
            src_ref=q_strips.at[:, t], dst_ref=q_turned.at[:, level(line)],
            send_sem=q_sem.at[0], recv_sem=q_sem.at[1], device_id={"line": t},
        ).start()

    over_line(send_state)
    own_state = pltpu.make_async_copy(
        q_strips.at[:, line], q_turned.at[:, level(line)], local_sem.at[1]
    )
    own_state.start()

    def part_state(v, carry):
        high, low = split(q[v].reshape(rows, LANES))
        q_both[v] = jnp.concatenate([high, low], 1)
        return carry

    lax.fori_loop(0, VARS, part_state, 0)

    own_request.wait()
    wait_for(req_in.at[pl.ds(0, groups - 1)], req_sem.at[1])
    asked = req_in[...].reshape(groups, LANES)
    for n in range(3 * capacity + VARS * VARS):
        told_all[n] = jnp.broadcast_to(asked[:, n:n + 1], (groups, LANES))
    cell_line = iota((groups, rows), 1).astype(f32)

    def wide(x):
        return jnp.concatenate([x] * (rows // LANES), 1) if rows >= LANES else x[:, :rows]

    def weigh(n, carry):
        share = wide(told_all[2 * capacity + n])
        high, low = split(
            jnp.where(cell_line == wide(told_all[n]), share, 0.0)
            + jnp.where(cell_line == wide(told_all[capacity + n]), 1.0 - share, 0.0)
        )
        choose[pl.ds(pl.multiple_of(n * groups, groups), groups)] = high
        choose[pl.ds(pl.multiple_of(named + n * groups, groups), groups)] = low
        return carry

    lax.fori_loop(0, capacity, weigh, 0)

    def interpolate(v, carry):
        both = dot(choose[...], q_both[v])
        lines[v] = (both[:named, :LANES] + both[:named, LANES:]) + both[named:, :LANES]
        return carry

    lax.fori_loop(0, VARS, interpolate, 0, unroll=True)

    def returned(g):
        return pl.ds(g * capacity, capacity)

    other_lines = pl.ds(0, named - capacity)

    def own_lines(a):
        return pltpu.make_async_copy(
            ret_out.at[a, zone], ret_in.at[a, returned(zone)], local_sem.at[2 + a]
        )

    def send_lines(a, carry):
        scale = [told_all[3 * capacity + a * VARS + v] for v in range(VARS)]
        for n in range(capacity):
            at = slice(n * groups, (n + 1) * groups)
            total = scale[0] * lines[0, at]
            for v in range(1, VARS):
                total += scale[v] * lines[v, at]
            ret_out[a, :, n] = total.reshape(groups, 1, LANES)

        def send(g):
            pltpu.make_async_remote_copy(
                src_ref=ret_out.at[a, g], dst_ref=ret_in.at[a, returned(zone)],
                send_sem=ret_send.at[a], recv_sem=ret_recv.at[a], device_id={"zone": g},
            ).start()

        over_zone(send)
        own_lines(a).start()
        return carry

    lax.fori_loop(0, VARS, send_lines, 0)

    moves[4].wait()
    slot_of = donor * capacity + position
    here = jnp.sum(
        jnp.where(
            iota((slots, padded), 1).astype(f32) == slot_of,
            column(receivers[...].astype(f32)) + 1.0,
            0.0,
        ),
        axis=0,
        keepdims=True,
    ) - 1.0
    place[...] = jnp.where(iota((rows, padded), 0).astype(f32) == here, 1.0, 0.0).astype(bf16)
    is_receiver[...] = jnp.broadcast_to(
        jnp.sum(
            jnp.where(iota((rows, slots), 0) == receivers[...], 1.0, 0.0), axis=1, keepdims=True
        ),
        (rows, LANES),
    )
    if padded > named:
        ret_in[:, named:] = jnp.zeros((VARS, padded - named, 1, LANES), f32)

    moves[5].wait()
    first_columns = right_columns(deriv[0].T)
    second_rows = left_rows(deriv[1])

    def derive(v, carry):
        both = dot(q_both[v], first_columns)
        ddx[v] = both[:, :LANES] + both[:, LANES:]
        state = q_both[v]
        stacked = jnp.concatenate(
            [
                jnp.concatenate([state[k * edge:(k + 1) * edge, n:n + LANES] for k in range(planes)], 1)
                for n in (0, LANES)
            ],
            0,
        )
        both = dot(second_rows, stacked)
        both = both[:edge] + both[edge:]
        for k in range(planes):
            ddy[v, k * edge:(k + 1) * edge] = both[:, k * LANES:(k + 1) * LANES]
        return carry

    lax.fori_loop(0, VARS, derive, 0)
    tile = min(32, edge)

    def mix_of(m, a, x):
        total = mix(m, a, 0) * x[0]
        for v in range(1, VARS):
            total += mix(m, a, v) * x[v]
        return total

    def residual(n, carry):
        at = pl.ds(pl.multiple_of(n * tile, tile), tile)
        plane = n // (edge // tile)
        inside = pl.ds(pl.multiple_of(lax.rem(n, edge // tile) * tile, tile), tile)
        active = line * planes + plane < size[0]
        x = [ddx[v, at] for v in range(VARS)]
        y = [ddy[v, at] for v in range(VARS)]
        taken = is_receiver[at]
        r = [
            jnp.where(active, -(mix_of(0, a, x) + mix_of(1, a, y)), 0.0) - taken * q[a, plane, inside]
            for a in range(VARS)
        ]
        for a in range(VARS):
            part[a, at] = mix_of(3, a, r)
        return carry

    lax.fori_loop(0, rows // tile, residual, 0)

    moves[6].wait()
    own_state.wait()
    wait_for(q_turned.at[:, others], q_sem.at[1])

    def whole_lines(ref, v):
        return jnp.concatenate(
            [ref[v, pl.ds(j, depth, stride=width), :] for j in range(width)], 1
        )

    third_rows = left_rows(deriv_z[...])

    def derive_z(v, carry):
        zed[v] = left_mul(third_rows, whole_lines(q_turned, v))
        return carry

    lax.fori_loop(0, VARS, derive_z, 0)
    levels = min(32, depth)

    def residual_z(n, carry):
        deep = lax.rem(n, depth // levels) * levels
        down = pl.ds(pl.multiple_of(deep, levels), levels)
        at = pl.ds(pl.multiple_of(n // (depth // levels) * LANES, LANES), LANES)
        active = iota((levels, LANES), 0) + deep < size[0]
        z = [zed[v, down, at] for v in range(VARS)]
        r = [jnp.where(active, -mix_of(2, a, z), 0.0) for a in range(VARS)]
        for a in range(VARS):
            mixed[a, down, at] = mix_of(3, a, r)
        return carry

    lax.fori_loop(0, width * (depth // levels), residual_z, 0)
    moves[7].wait()
    moves[8].wait()

    def prepare(v, carry):
        rows_z[v] = left_rows(inverse_z[v])
        rows_y[v] = left_rows(inverse[1, v])
        columns_x[v] = right_columns(inverse[0, v].T)
        return carry

    lax.fori_loop(0, VARS, prepare, 0)

    def add_source(a):
        own_lines(a).wait()
        wait_for(ret_in.at[a, other_lines], ret_recv.at[a])
        high, low = split(ret_in[a].reshape(padded, LANES))
        both = dot(place[...], jnp.concatenate([high, low], 1))
        part_strips[a] = strips(part[a] + (both[:, :LANES] + both[:, LANES:]))

        def send_part(t):
            pltpu.make_async_remote_copy(
                src_ref=part_strips.at[a, t], dst_ref=part_turned.at[a, level(line)],
                send_sem=part_send.at[a], recv_sem=part_recv.at[a], device_id={"line": t},
            ).start()

        over_line(send_part)
        part_turned[a, level(line)] = part_strips[a, line]

    def solve_z(a):
        wait_for(part_turned.at[a, others], part_recv.at[a])
        solved = left_mul(rows_z[a], whole_lines(part_turned, a) + mixed[a])
        for j in range(width):
            turned_back[a, pl.ds(j, depth, stride=width), :] = solved[:, j * LANES:(j + 1) * LANES]

        def send_back(t):
            pltpu.make_async_remote_copy(
                src_ref=turned_back.at[a, level(t)], dst_ref=back.at[a, line],
                send_sem=back_send.at[a], recv_sem=back_recv.at[a], device_id={"line": t},
            ).start()

        over_line(send_back)
        back[a, line] = turned_back[a, level(line)]

    def source_and_solve(a, carry):
        @pl.when(a < VARS)
        def _():
            add_source(a)

        @pl.when(a > 0)
        def _():
            solve_z(a - 1)

        return carry

    lax.fori_loop(0, VARS + 1, source_and_solve, 0)

    for a in range(VARS - 1):
        wait_for(turned_back.at[a, others], back_recv.at[a])
    last = VARS - 1
    strip_tile = min(4, blocks)

    def all_but_last(n, carry):
        at = pl.ds(n * strip_tile, strip_tile)
        x = [back[a, at] for a in range(last)]
        for v in range(VARS):
            total = mix(4, v, 0) * x[0]
            for a in range(1, last):
                total += mix(4, v, a) * x[a]
            step_b[v, at] = total
        return carry

    lax.fori_loop(0, blocks // strip_tile, all_but_last, 0)
    wait_for(turned_back.at[last, others], back_recv.at[last])

    def solve_y(v, carry):
        x = step_b[v] + mixers[v, last, 4] * back[last]
        x = jnp.concatenate(
            [x[:, k * width:(k + 1) * width, :].reshape(edge, LANES) for k in range(planes)], 1
        )
        both = left_mul(rows_y[v], x)
        for k in range(planes):
            step_a[v, k * edge:(k + 1) * edge] = both[:, k * LANES:(k + 1) * LANES]
        return carry

    lax.fori_loop(0, VARS, solve_y, 0, unroll=True)

    def mix_second(n, carry):
        at = pl.ds(pl.multiple_of(n * tile, tile), tile)
        x = [step_a[v, at] for v in range(VARS)]
        for a in range(VARS):
            ddx[a, at] = mix_of(5, a, x)
        return carry

    lax.fori_loop(0, rows // tile, mix_second, 0)

    def solve_x(v, carry):
        ddy[v] = right_mul(ddx[v], columns_x[v])
        return carry

    lax.fori_loop(0, VARS, solve_x, 0, unroll=True)

    def mix_last(n, carry):
        at = pl.ds(pl.multiple_of(n * tile, tile), tile)
        inside = pl.ds(pl.multiple_of(lax.rem(n, edge // tile) * tile, tile), tile)
        x = [ddy[v, at] for v in range(VARS)]
        for a in range(VARS):
            out[a, n // (edge // tile), inside] = mix_of(6, a, x)
        return carry

    lax.fori_loop(0, rows // tile, mix_last, 0)

    wait_for(req_in.at[pl.ds(0, groups - 1)], req_sem.at[0])
    wait_for(q_turned.at[:, others], q_sem.at[0])
    for a in range(VARS):
        wait_for(ret_in.at[a, other_lines], ret_send.at[a])
        wait_for(part_turned.at[a, others], part_send.at[a])
        wait_for(turned_back.at[a, others], back_send.at[a])


def local(
    flow_state, derivative, derivative_z, line_inverse, line_inverse_z, mixers, zone_size,
    receiver_line, donor_group, donor_line, stencil_weight,
):
    groups, blocks = lax.axis_size("zone"), lax.axis_size("line")
    planes, edge = flow_state.shape[2], flow_state.shape[3]
    slots = receiver_line.shape[2]
    capacity = max(2, 5 * slots // (2 * groups))
    rows, depth, width = planes * edge, planes * blocks, edge // blocks
    named = groups * capacity
    padded = -(-named // LANES) * LANES
    dma = pltpu.SemaphoreType.DMA
    vmem = pl.BlockSpec(memory_space=pltpu.VMEM)
    hbm = pl.BlockSpec(memory_space=pltpu.HBM)
    smem = pl.BlockSpec(memory_space=pltpu.SMEM)
    result = pl.pallas_call(
        functools.partial(kernel, capacity),
        out_shape=jax.ShapeDtypeStruct((VARS, planes, edge, LANES), f32),
        in_specs=[hbm] * 5 + [smem] * 2 + [hbm] * 4,
        out_specs=vmem,
        scratch_shapes=[
            pltpu.VMEM((VARS, planes, edge, LANES), f32),
            pltpu.VMEM(derivative.shape, f32),
            pltpu.VMEM(derivative_z.shape, f32),
            pltpu.VMEM(line_inverse.shape[1:], f32),
            pltpu.VMEM(line_inverse_z.shape[1:], f32),
            pltpu.VMEM((1, slots), jnp.int32),
            pltpu.VMEM((1, slots), jnp.int32),
            pltpu.VMEM((2, slots), jnp.int32),
            pltpu.VMEM((1, slots), f32),
            pltpu.VMEM((groups, 1, LANES), f32),
            pltpu.VMEM((groups, 1, LANES), f32),
            pltpu.VMEM((3 * capacity + VARS * VARS, groups, LANES), f32),
            pltpu.VMEM((VARS, blocks, planes * width, LANES), f32),
            pltpu.VMEM((VARS, rows, 2 * LANES), bf16),
            pltpu.VMEM((VARS, depth * width, LANES), f32),
            pltpu.VMEM((VARS, rows, LANES), f32),
            pltpu.VMEM((VARS, rows, LANES), f32),
            pltpu.VMEM((VARS, rows, LANES), f32),
            pltpu.VMEM((VARS, blocks, planes * width, LANES), f32),
            pltpu.VMEM((rows, LANES), f32),
            pltpu.VMEM((VARS, named, LANES), f32),
            pltpu.VMEM((VARS, groups, capacity, 1, LANES), f32),
            pltpu.VMEM((VARS, padded, 1, LANES), f32),
            pltpu.VMEM((2 * named, rows), bf16),
            pltpu.VMEM((rows, padded), bf16),
            pltpu.VMEM((VARS, 2 * depth, 2 * depth), bf16),
            pltpu.VMEM((VARS, 2 * edge, 2 * edge), bf16),
            pltpu.VMEM((VARS, 2 * LANES, 2 * LANES), bf16),
            pltpu.VMEM((VARS, depth * width, LANES), f32),
            pltpu.VMEM((VARS, depth, width * LANES), f32),
            pltpu.VMEM((VARS, depth, width * LANES), f32),
            pltpu.VMEM((VARS, depth * width, LANES), f32),
            pltpu.VMEM((VARS, blocks, planes * width, LANES), f32),
            pltpu.VMEM((VARS, rows, LANES), f32),
            pltpu.VMEM((VARS, blocks, planes * width, LANES), f32),
            dma((9,)),
            dma((2 + VARS,)),
            dma((2,)),
            dma((2,)),
        ] + [dma((VARS,))] * 6,
        compiler_params=pltpu.CompilerParams(
            collective_id=0, has_side_effects=True, vmem_limit_bytes=48 * 2**20
        ),
    )(
        *(pltpu.with_memory_space_constraint(x, pltpu.HBM) for x in (flow_state[0], derivative, derivative_z, line_inverse[0], line_inverse_z[0])),
        jnp.transpose(mixers[0], (1, 2, 0)), zone_size,
        *(pltpu.with_memory_space_constraint(x, pltpu.HBM) for x in (receiver_line[0], donor_group[0, :, :, 0], donor_line[0, 0].T, stencil_weight[0])),
    )
    return result[None]


def solution(mesh):
    placed = (
        P("zone", None, "line", None, None),
        P(),
        P(),
        P("zone", None, None, None, None),
        P("zone", None, None, None),
        P("zone", None, None, None),
        P("zone"),
        P("zone", "line", None),
        P("zone", "line", None, None),
        P("zone", "line", None, None),
        P("zone", "line", None),
    )
    return jax.shard_map(
        local,
        mesh=mesh,
        in_specs=placed,
        out_specs=P("zone", None, "line", None, None),
        check_vma=False,
    )
```

```python
import functools

import jax
import jax.numpy as jnp
from jax import lax
from jax.experimental import pallas as pl
from jax.experimental.pallas import tpu as pltpu
from jax.sharding import PartitionSpec as P

f32 = jnp.float32
bf16 = jnp.bfloat16
VARS = 5
LANES = 128


def split(x):
    high = x.astype(bf16)
    return high, (x - high.astype(f32)).astype(bf16)


def dot(a, b):
    return jnp.dot(a, b, preferred_element_type=f32)


def left_rows(w):
    high, low = split(w)
    return jnp.concatenate(
        [jnp.concatenate([high, high], 1), jnp.concatenate([low, jnp.zeros_like(low)], 1)], 0
    )


def left_mul(rows, x):
    high, low = split(x)
    both = dot(rows, jnp.concatenate([high, low], 0))
    half = x.shape[0]
    return both[:half] + both[half:]


def right_columns(w):
    high, low = split(w)
    return jnp.concatenate(
        [jnp.concatenate([high, low], 1), jnp.concatenate([high, jnp.zeros_like(low)], 1)], 0
    )


def right_mul(x, columns):
    high, low = split(x)
    both = dot(jnp.concatenate([high, low], 1), columns)
    half = columns.shape[1] // 2
    return both[:, :half] + both[:, half:]


def pick(rows, x):
    first, rest = split(x)
    rest = x - first.astype(f32)
    second = rest.astype(bf16)
    third = (rest - second.astype(f32)).astype(bf16)
    return (dot(rows, first) + dot(rows, second)) + dot(rows, third)


def iota(shape, axis):
    return lax.broadcasted_iota(jnp.int32, shape, axis)


def kernel(
    capacity,
    q_hbm, deriv_hbm, deriv_z_hbm, inverse_hbm, inverse_z_hbm, mixers, size,
    receivers_hbm, donors_hbm, pairs_hbm, weights_hbm,
    out,
    q, deriv, deriv_z, inverse, inverse_z, receivers, donors, pairs, weights,
    req_out, req_in, told_all, q_strips, q_both, q_turned, ddx, ddy, part, part_strips, is_receiver,
    lines, ret_out, ret_in, choose, place, rows_z, rows_y, columns_x,
    part_turned, zed, mixed, turned_back, back, step_a, step_b,
    load_sem, local_sem, req_sem, q_sem,
    ret_send, ret_recv, part_send, part_recv, back_send, back_recv,
):
    groups, blocks = lax.axis_size("zone"), lax.axis_size("line")
    zone, line = lax.axis_index("zone"), lax.axis_index("line")

    def mix(m, a, v):
        return mixers[a, v, m]

    moves = [
        pltpu.make_async_copy(source, target, load_sem.at[n])
        for n, (source, target) in enumerate((
            (donors_hbm, donors), (pairs_hbm, pairs), (weights_hbm, weights), (q_hbm, q),
            (receivers_hbm, receivers), (deriv_hbm, deriv), (deriv_z_hbm, deriv_z),
            (inverse_z_hbm, inverse_z), (inverse_hbm, inverse),
        ))
    ]
    for move in moves[:3]:
        move.start()
    planes, edge = q.shape[1], q.shape[2]
    rows = planes * edge
    depth = planes * blocks
    width = edge // blocks
    slots = receivers.shape[1]
    piece = planes * width
    named = groups * capacity
    padded = ret_in.shape[1]

    def over_zone(body):
        def step(n, carry):
            turn = lax.rem(n, 2)
            offset = groups // 2 + (n + turn) // 2 * (2 * turn - 1)
            body(lax.rem(zone + (offset if groups % 2 == 0 else n + 1), groups))
            return carry

        lax.fori_loop(0, groups - 1, step, 0)

    side = next((n for n in (2, 3, 4, 8) if n * n == blocks), 1)
    tall = blocks // side

    def hops(step):
        return min(step[0], tall - step[0]) + min(step[1], side - step[1])

    steps = sorted(
        ((y, x) for y in range(tall) for x in range(side) if (y, x) != (0, 0)),
        key=lambda step: (-hops(step), sorted((min(step[0], tall - step[0]), min(step[1], side - step[1])))),
    )

    def over_line(body):
        for y, x in steps:
            body(lax.rem(line // side + y, tall) * side + lax.rem(line + x, side))

    def strips(x):
        x = x.reshape(planes, blocks, width, LANES)
        return jnp.swapaxes(x, 0, 1).reshape(blocks, piece, LANES)

    def level(t):
        return pl.ds(pl.multiple_of(t * piece, piece), piece)

    others = pl.ds(0, (blocks - 1) * piece)

    def wait_for(ref, sem):
        pltpu.make_async_copy(ref, ref, sem).wait()

    barrier = pltpu.get_barrier_semaphore()
    over_zone(lambda g: pl.semaphore_signal(barrier, inc=1, device_id={"zone": g}))
    over_line(lambda t: pl.semaphore_signal(barrier, inc=1, device_id={"line": t}))
    for move in moves[3:]:
        move.start()

    diagonal = iota((slots, slots), 0) == iota((slots, slots), 1)

    def column(row):
        return jnp.sum(jnp.where(diagonal, row, 0.0), axis=1, keepdims=True)

    for move in moves[:3]:
        move.wait()
    donor_row = donors[...].astype(f32)
    donor = column(donor_row)
    same_before = (donor == donor_row) & (iota((slots, slots), 1) < iota((slots, slots), 0))
    position = jnp.sum(jnp.where(same_before, 1.0, 0.0), axis=1, keepdims=True)
    lane = iota((slots, LANES), 1).astype(f32)
    line_pair = pairs[...].astype(f32)
    told = (
        jnp.where(lane == position, column(line_pair[0:1]), 0.0)
        + jnp.where(lane == position + capacity, column(line_pair[1:2]), 0.0)
        + jnp.where(lane == position + 2 * capacity, column(weights[...]), 0.0)
    )
    asks = jnp.where(iota((groups, slots), 0).astype(f32) == donor_row, 1.0, 0.0).astype(bf16)
    own_mixer = jnp.zeros((1, LANES), f32)
    for n in range(VARS * VARS):
        at = iota((1, LANES), 1) == 3 * capacity + n
        own_mixer = jnp.where(at, mixers[n // VARS, n % VARS, 3], own_mixer)
    req_out[...] = (pick(asks, told) + own_mixer).reshape(groups, 1, LANES)

    pl.semaphore_wait(barrier, groups + blocks - 2)

    def send_request(g):
        pltpu.make_async_remote_copy(
            src_ref=req_out.at[g], dst_ref=req_in.at[zone],
            send_sem=req_sem.at[0], recv_sem=req_sem.at[1], device_id={"zone": g},
        ).start()

    over_zone(send_request)
    own_request = pltpu.make_async_copy(req_out.at[zone], req_in.at[zone], local_sem.at[0])
    own_request.start()
    moves[3].wait()

    def cut_state(v, carry):
        q_strips[v] = strips(q[v])
        return carry

    lax.fori_loop(0, VARS, cut_state, 0)

    def send_state(t):
        pltpu.make_async_remote_copy(
            src_ref=q_strips.at[:, t], dst_ref=q_turned.at[:, level(line)],
            send_sem=q_sem.at[0], recv_sem=q_sem.at[1], device_id={"line": t},
        ).start()

    over_line(send_state)
    own_state = pltpu.make_async_copy(
        q_strips.at[:, line], q_turned.at[:, level(line)], local_sem.at[1]
    )
    own_state.start()

    def part_state(v, carry):
        high, low = split(q[v].reshape(rows, LANES))
        q_both[v] = jnp.concatenate([high, low], 1)
        return carry

    lax.fori_loop(0, VARS, part_state, 0)

    own_request.wait()
    wait_for(req_in.at[pl.ds(0, groups - 1)], req_sem.at[1])
    asked = req_in[...].reshape(groups, LANES)
    for n in range(3 * capacity + VARS * VARS):
        told_all[n] = jnp.broadcast_to(asked[:, n:n + 1], (groups, LANES))
    cell_line = iota((groups, rows), 1).astype(f32)

    def wide(x):
        return jnp.concatenate([x] * (rows // LANES), 1) if rows >= LANES else x[:, :rows]

    def weigh(n, carry):
        share = wide(told_all[2 * capacity + n])
        high, low = split(
            jnp.where(cell_line == wide(told_all[n]), share, 0.0)
            + jnp.where(cell_line == wide(told_all[capacity + n]), 1.0 - share, 0.0)
        )
        choose[pl.ds(pl.multiple_of(n * groups, groups), groups)] = high
        choose[pl.ds(pl.multiple_of(named + n * groups, groups), groups)] = low
        return carry

    lax.fori_loop(0, capacity, weigh, 0)

    def interpolate(v, carry):
        both = dot(choose[...], q_both[v])
        lines[v] = (both[:named, :LANES] + both[:named, LANES:]) + both[named:, :LANES]
        return carry

    lax.fori_loop(0, VARS, interpolate, 0, unroll=True)

    def returned(g):
        return pl.ds(g * capacity, capacity)

    other_lines = pl.ds(0, named - capacity)

    def own_lines(a):
        return pltpu.make_async_copy(
            ret_out.at[a, zone], ret_in.at[a, returned(zone)], local_sem.at[2 + a]
        )

    def send_lines(a, carry):
        scale = [told_all[3 * capacity + a * VARS + v] for v in range(VARS)]
        for n in range(capacity):
            at = slice(n * groups, (n + 1) * groups)
            total = scale[0] * lines[0, at]
            for v in range(1, VARS):
                total += scale[v] * lines[v, at]
            ret_out[a, :, n] = total.reshape(groups, 1, LANES)

        def send(g):
            pltpu.make_async_remote_copy(
                src_ref=ret_out.at[a, g], dst_ref=ret_in.at[a, returned(zone)],
                send_sem=ret_send.at[a], recv_sem=ret_recv.at[a], device_id={"zone": g},
            ).start()

        over_zone(send)
        own_lines(a).start()
        return carry

    lax.fori_loop(0, VARS, send_lines, 0)

    moves[4].wait()
    slot_of = donor * capacity + position
    here = jnp.sum(
        jnp.where(
            iota((slots, padded), 1).astype(f32) == slot_of,
            column(receivers[...].astype(f32)) + 1.0,
            0.0,
        ),
        axis=0,
        keepdims=True,
    ) - 1.0
    place[...] = jnp.where(iota((rows, padded), 0).astype(f32) == here, 1.0, 0.0).astype(bf16)
    is_receiver[...] = jnp.broadcast_to(
        jnp.sum(
            jnp.where(iota((rows, slots), 0) == receivers[...], 1.0, 0.0), axis=1, keepdims=True
        ),
        (rows, LANES),
    )
    if padded > named:
        ret_in[:, named:] = jnp.zeros((VARS, padded - named, 1, LANES), f32)

    moves[5].wait()
    first_columns = right_columns(deriv[0].T)
    second_rows = left_rows(deriv[1])

    def derive(v, carry):
        both = dot(q_both[v], first_columns)
        ddx[v] = both[:, :LANES] + both[:, LANES:]
        state = q_both[v]
        stacked = jnp.concatenate(
            [
                jnp.concatenate([state[k * edge:(k + 1) * edge, n:n + LANES] for k in range(planes)], 1)
                for n in (0, LANES)
            ],
            0,
        )
        both = dot(second_rows, stacked)
        both = both[:edge] + both[edge:]
        for k in range(planes):
            ddy[v, k * edge:(k + 1) * edge] = both[:, k * LANES:(k + 1) * LANES]
        return carry

    lax.fori_loop(0, VARS, derive, 0)
    tile = min(32, edge)

    def mix_of(m, a, x):
        total = mix(m, a, 0) * x[0]
        for v in range(1, VARS):
            total += mix(m, a, v) * x[v]
        return total

    def residual(n, carry):
        at = pl.ds(pl.multiple_of(n * tile, tile), tile)
        plane = n // (edge // tile)
        inside = pl.ds(pl.multiple_of(lax.rem(n, edge // tile) * tile, tile), tile)
        active = line * planes + plane < size[0]
        x = [ddx[v, at] for v in range(VARS)]
        y = [ddy[v, at] for v in range(VARS)]
        taken = is_receiver[at]
        r = [
            jnp.where(active, -(mix_of(0, a, x) + mix_of(1, a, y)), 0.0) - taken * q[a, plane, inside]
            for a in range(VARS)
        ]
        for a in range(VARS):
            part[a, at] = mix_of(3, a, r)
        return carry

    lax.fori_loop(0, rows // tile, residual, 0)

    moves[6].wait()
    own_state.wait()
    wait_for(q_turned.at[:, others], q_sem.at[1])

    def whole_lines(ref, v):
        return jnp.concatenate(
            [ref[v, pl.ds(j, depth, stride=width), :] for j in range(width)], 1
        )

    third_rows = left_rows(deriv_z[...])

    def derive_z(v, carry):
        zed[v] = left_mul(third_rows, whole_lines(q_turned, v))
        return carry

    lax.fori_loop(0, VARS, derive_z, 0)
    levels = min(32, depth)

    def residual_z(n, carry):
        deep = lax.rem(n, depth // levels) * levels
        down = pl.ds(pl.multiple_of(deep, levels), levels)
        at = pl.ds(pl.multiple_of(n // (depth // levels) * LANES, LANES), LANES)
        active = iota((levels, LANES), 0) + deep < size[0]
        z = [zed[v, down, at] for v in range(VARS)]
        r = [jnp.where(active, -mix_of(2, a, z), 0.0) for a in range(VARS)]
        for a in range(VARS):
            mixed[a, down, at] = mix_of(3, a, r)
        return carry

    lax.fori_loop(0, width * (depth // levels), residual_z, 0)
    moves[7].wait()
    moves[8].wait()

    def prepare(v, carry):
        rows_z[v] = left_rows(inverse_z[v])
        rows_y[v] = left_rows(inverse[1, v])
        columns_x[v] = right_columns(inverse[0, v].T)
        return carry

    lax.fori_loop(0, VARS, prepare, 0)

    def add_source(a):
        own_lines(a).wait()
        wait_for(ret_in.at[a, other_lines], ret_recv.at[a])
        high, low = split(ret_in[a].reshape(padded, LANES))
        both = dot(place[...], jnp.concatenate([high, low], 1))
        part_strips[a] = strips(part[a] + (both[:, :LANES] + both[:, LANES:]))

        def send_part(t):
            pltpu.make_async_remote_copy(
                src_ref=part_strips.at[a, t], dst_ref=part_turned.at[a, level(line)],
                send_sem=part_send.at[a], recv_sem=part_recv.at[a], device_id={"line": t},
            ).start()

        over_line(send_part)
        part_turned[a, level(line)] = part_strips[a, line]

    def solve_z(a):
        wait_for(part_turned.at[a, others], part_recv.at[a])
        solved = left_mul(rows_z[a], whole_lines(part_turned, a) + mixed[a])
        for j in range(width):
            turned_back[a, pl.ds(j, depth, stride=width), :] = solved[:, j * LANES:(j + 1) * LANES]

        def send_back(t):
            pltpu.make_async_remote_copy(
                src_ref=turned_back.at[a, level(t)], dst_ref=back.at[a, line],
                send_sem=back_send.at[a], recv_sem=back_recv.at[a], device_id={"line": t},
            ).start()

        over_line(send_back)
        back[a, line] = turned_back[a, level(line)]

    def source_and_solve(a, carry):
        @pl.when(a < VARS)
        def _():
            add_source(a)

        @pl.when(a > 0)
        def _():
            solve_z(a - 1)

        return carry

    lax.fori_loop(0, VARS + 1, source_and_solve, 0)

    for a in range(VARS - 1):
        wait_for(turned_back.at[a, others], back_recv.at[a])
    last = VARS - 1
    strip_tile = min(4, blocks)

    def all_but_last(n, carry):
        at = pl.ds(n * strip_tile, strip_tile)
        x = [back[a, at] for a in range(last)]
        for v in range(VARS):
            total = mix(4, v, 0) * x[0]
            for a in range(1, last):
                total += mix(4, v, a) * x[a]
            step_b[v, at] = total
        return carry

    lax.fori_loop(0, blocks // strip_tile, all_but_last, 0)
    wait_for(turned_back.at[last, others], back_recv.at[last])

    def solve_y(v, carry):
        x = step_b[v] + mixers[v, last, 4] * back[last]
        x = jnp.concatenate(
            [x[:, k * width:(k + 1) * width, :].reshape(edge, LANES) for k in range(planes)], 1
        )
        both = left_mul(rows_y[v], x)
        for k in range(planes):
            step_a[v, k * edge:(k + 1) * edge] = both[:, k * LANES:(k + 1) * LANES]
        return carry

    lax.fori_loop(0, VARS, solve_y, 0, unroll=True)

    def mix_second(n, carry):
        at = pl.ds(pl.multiple_of(n * tile, tile), tile)
        x = [step_a[v, at] for v in range(VARS)]
        for a in range(VARS):
            ddx[a, at] = mix_of(5, a, x)
        return carry

    lax.fori_loop(0, rows // tile, mix_second, 0)

    def solve_x(v, carry):
        ddy[v] = right_mul(ddx[v], columns_x[v])
        return carry

    lax.fori_loop(0, VARS, solve_x, 0, unroll=True)

    def mix_last(n, carry):
        at = pl.ds(pl.multiple_of(n * tile, tile), tile)
        inside = pl.ds(pl.multiple_of(lax.rem(n, edge // tile) * tile, tile), tile)
        x = [ddy[v, at] for v in range(VARS)]
        for a in range(VARS):
            out[a, n // (edge // tile), inside] = mix_of(6, a, x)
        return carry

    lax.fori_loop(0, rows // tile, mix_last, 0)

    wait_for(req_in.at[pl.ds(0, groups - 1)], req_sem.at[0])
    wait_for(q_turned.at[:, others], q_sem.at[0])
    for a in range(VARS):
        wait_for(ret_in.at[a, other_lines], ret_send.at[a])
        wait_for(part_turned.at[a, others], part_send.at[a])
        wait_for(turned_back.at[a, others], back_send.at[a])


def local(
    flow_state, derivative, derivative_z, line_inverse, line_inverse_z, mixers, zone_size,
    receiver_line, donor_group, donor_line, stencil_weight,
):
    groups, blocks = lax.axis_size("zone"), lax.axis_size("line")
    planes, edge = flow_state.shape[2], flow_state.shape[3]
    slots = receiver_line.shape[2]
    capacity = max(2, 5 * slots // (2 * groups))
    rows, depth, width = planes * edge, planes * blocks, edge // blocks
    named = groups * capacity
    padded = -(-named // LANES) * LANES
    dma = pltpu.SemaphoreType.DMA
    vmem = pl.BlockSpec(memory_space=pltpu.VMEM)
    hbm = pl.BlockSpec(memory_space=pltpu.HBM)
    smem = pl.BlockSpec(memory_space=pltpu.SMEM)
    result = pl.pallas_call(
        functools.partial(kernel, capacity),
        out_shape=jax.ShapeDtypeStruct((VARS, planes, edge, LANES), f32),
        in_specs=[hbm] * 5 + [smem] * 2 + [hbm] * 4,
        out_specs=vmem,
        scratch_shapes=[
            pltpu.VMEM((VARS, planes, edge, LANES), f32),
            pltpu.VMEM(derivative.shape, f32),
            pltpu.VMEM(derivative_z.shape, f32),
            pltpu.VMEM(line_inverse.shape[1:], f32),
            pltpu.VMEM(line_inverse_z.shape[1:], f32),
            pltpu.VMEM((1, slots), jnp.int32),
            pltpu.VMEM((1, slots), jnp.int32),
            pltpu.VMEM((2, slots), jnp.int32),
            pltpu.VMEM((1, slots), f32),
            pltpu.VMEM((groups, 1, LANES), f32),
            pltpu.VMEM((groups, 1, LANES), f32),
            pltpu.VMEM((3 * capacity + VARS * VARS, groups, LANES), f32),
            pltpu.VMEM((VARS, blocks, planes * width, LANES), f32),
            pltpu.VMEM((VARS, rows, 2 * LANES), bf16),
            pltpu.VMEM((VARS, depth * width, LANES), f32),
            pltpu.VMEM((VARS, rows, LANES), f32),
            pltpu.VMEM((VARS, rows, LANES), f32),
            pltpu.VMEM((VARS, rows, LANES), f32),
            pltpu.VMEM((VARS, blocks, planes * width, LANES), f32),
            pltpu.VMEM((rows, LANES), f32),
            pltpu.VMEM((VARS, named, LANES), f32),
            pltpu.VMEM((VARS, groups, capacity, 1, LANES), f32),
            pltpu.VMEM((VARS, padded, 1, LANES), f32),
            pltpu.VMEM((2 * named, rows), bf16),
            pltpu.VMEM((rows, padded), bf16),
            pltpu.VMEM((VARS, 2 * depth, 2 * depth), bf16),
            pltpu.VMEM((VARS, 2 * edge, 2 * edge), bf16),
            pltpu.VMEM((VARS, 2 * LANES, 2 * LANES), bf16),
            pltpu.VMEM((VARS, depth * width, LANES), f32),
            pltpu.VMEM((VARS, depth, width * LANES), f32),
            pltpu.VMEM((VARS, depth, width * LANES), f32),
            pltpu.VMEM((VARS, depth * width, LANES), f32),
            pltpu.VMEM((VARS, blocks, planes * width, LANES), f32),
            pltpu.VMEM((VARS, rows, LANES), f32),
            pltpu.VMEM((VARS, blocks, planes * width, LANES), f32),
            dma((9,)),
            dma((2 + VARS,)),
            dma((2,)),
            dma((2,)),
        ] + [dma((VARS,))] * 6,
        compiler_params=pltpu.CompilerParams(
            collective_id=0, has_side_effects=True, vmem_limit_bytes=48 * 2**20
        ),
    )(
        *(pltpu.with_memory_space_constraint(x, pltpu.HBM) for x in (flow_state[0], derivative, derivative_z, line_inverse[0], line_inverse_z[0])),
        jnp.transpose(mixers[0], (1, 2, 0)), zone_size,
        *(pltpu.with_memory_space_constraint(x, pltpu.HBM) for x in (receiver_line[0], donor_group[0, :, :, 0], donor_line[0, 0].T, stencil_weight[0])),
    )
    return result[None]


def solution(mesh):
    placed = (
        P("zone", None, "line", None, None),
        P(),
        P(),
        P("zone", None, None, None, None),
        P("zone", None, None, None),
        P("zone", None, None, None),
        P("zone"),
        P("zone", "line", None),
        P("zone", "line", None, None),
        P("zone", "line", None, None),
        P("zone", "line", None),
    )
    return jax.shard_map(
        local,
        mesh=mesh,
        in_specs=placed,
        out_specs=P("zone", None, "line", None, None),
        check_vma=False,
    )
```
